128 devices in a mesh: tgt: 16 (over y_hi, z, core), sup: 8 (over y_lo, x).
Axes of the slice: x: 4, y: 4 (y_hi: 2, y_lo: 2; y = y_hi * 2 + y_lo), z: 4, core: 2. Of those that a mesh axis runs over, the one named last changes fastest.
Arguments:
- target_pool: float32 [1024, 3, 1024], P('tgt'), may hold values from -6 to 6
- target_index: int32 [128], P('tgt'), may hold values from 0 to 1023, as said below
- target_labels: int32 [128], P('tgt'), may hold values from 0 to 99
- dual_weights: float32 [512, 100], P('sup'), may hold values from -0.25 to 0.25
- support_images: float32 [512, 3, 1024], P(('sup', 'tgt')), may hold values from -6 to 6
Outputs:
- residual: float32 [128, 100], P('tgt')
- support_grad: float32 [512, 3, 1024], P(('sup', 'tgt'))
The draws below stay inside these ranges and needn't reach their ends.
Inputs may be any that keep to these rules, and one draw needn't show every extreme that they name: `target_index`: for each j, the targets 8 * j to 8 * (j + 1) - 1 name distinct candidates among 64 * j to 64 * (j + 1) - 1.
All inputs are finite; a program needn't handle non-finite values.
Results may differ from the reference program's by a relative error of at most 0.0003.
Values sent between devices are 32-bit elements; how exact they have to be, the bound alone decides.
No kernel may reach another device: no remote copies, remote signals or barrier semaphores. Data moves between devices by JAX's collectives and lax.ppermute only.
A program may use at most 64 MiB of HBM per device.

```python
import math
import jax
import jax.numpy as jnp
from jax import lax

CHANNELS = 3
SIDE = 32
CLASSES = 100
LAYERS = 3
TGT_DEV = 8
POOL_DEV = 64
PIXELS = 1024
TARGETS = 128
SUPPORT = 512
POOL = 1024


def draw_target_index(key, part):
    blocks = TARGETS // TGT_DEV
    block_keys = jax.random.split(key, blocks)
    block_ids = jnp.arange(blocks)

    def one_block(block_key, block_id):
        first_key, second_key, third_key = jax.random.split(block_key, 3)
        drawn = jax.random.permutation(first_key, POOL_DEV)[:TGT_DEV]
        others = jax.random.permutation(second_key, POOL_DEV - 1)[:TGT_DEV - 1]
        with_low = jnp.concatenate([others + 1, jnp.zeros((1,), jnp.int32)])
        with_high = jnp.concatenate([others, jnp.full((1,), POOL_DEV - 1, jnp.int32)])
        picked = jnp.where(block_id == 0, with_low, jnp.where(block_id == blocks - 1, with_high, drawn.astype(jnp.int32)))
        order = jax.random.permutation(third_key, TGT_DEV)
        return jnp.take(picked, order)
    chosen = jax.vmap(one_block)(block_keys, block_ids)
    offsets = (block_ids * POOL_DEV)[:, None]
    return (chosen + offsets).reshape(-1).astype(jnp.int32)


def place_ends(array, own_key, low, high):
    index_at = [jax.random.randint(jax.random.fold_in(own_key, axis), (), 0, length) for axis, length in enumerate(array.shape)]
    longest = array.shape.index(max(array.shape))
    beside = index_at[:longest] + [(index_at[longest] + 1) % array.shape[longest]] + index_at[longest + 1:]
    return array.at[tuple(index_at)].set(low).at[tuple(beside)].set(high)


def block_scale(rng, shape, cuts, least, top_value):
    def one(axis_at, blocks):
        steps = jax.random.uniform(jax.random.fold_in(jax.random.fold_in(rng, 6), axis_at), (blocks,), jnp.float32, least / len(cuts), top_value / len(cuts))
        return jnp.repeat(jnp.exp(steps), shape[axis_at] // blocks).reshape((-1,) + (1,) * (len(shape) - axis_at - 1))

    gain = one(*cuts[0])
    for cut in cuts[1:]:
        gain = gain * one(*cut)
    return gain


def noise(key, dims, width, bound, pieces=(), kind=jnp.bfloat16):
    values = jax.random.normal(key, dims, jnp.float32) * width
    if len(pieces) > 0:
        values = block_scale(key, dims, pieces, -0.22, 0.18) * values
    return jnp.clip(values, min=-bound, max=bound).astype(kind)


def setup_inputs(seed: int = 0) -> dict:
    seeds = jax.random.split(jax.random.key(seed), 6)
    target_pool = noise(seeds[0], (POOL, CHANNELS, PIXELS), 1.0, 6.0, ((0, 16),), jnp.float32)
    target_index = draw_target_index(jax.random.fold_in(seeds[5], 71), 0)
    target_labels = place_ends(jax.random.randint(seeds[2], (TARGETS,), 0, CLASSES), jax.random.fold_in(seeds[2], 1), 0, CLASSES - 1).astype(jnp.int32)
    dual_weights = noise(seeds[3], (SUPPORT, CLASSES), SUPPORT ** -0.5, 0.25, ((0, 8),), jnp.float32)
    support_images = noise(seeds[4], (SUPPORT, CHANNELS, PIXELS), 1.0, 6.0, ((0, 128),), jnp.float32)
    return {"target_pool": target_pool, "target_index": target_index, "target_labels": target_labels, "dual_weights": dual_weights, "support_images": support_images}


bias_variance = 0.01

def box_filter(pixel_map):
    column = jnp.arange(PIXELS) % SIDE
    zero_column = jnp.zeros(pixel_map.shape[:-1] + (1,), pixel_map.dtype)
    shifted_right = jnp.concatenate([zero_column, pixel_map[..., :-1]], axis=-1)
    shifted_left = jnp.concatenate([pixel_map[..., 1:], zero_column], axis=-1)
    across = pixel_map + jnp.where(column > 0, shifted_right, 0.0) + jnp.where(column < SIDE - 1, shifted_left, 0.0)
    zero_row = jnp.zeros(pixel_map.shape[:-1] + (SIDE,), pixel_map.dtype)
    shifted_down = jnp.concatenate([zero_row, across[..., :-SIDE]], axis=-1)
    shifted_up = jnp.concatenate([across[..., SIDE:], zero_row], axis=-1)
    return (across + shifted_down + shifted_up) / 9.0

def self_maps(images):
    energy = images[:, 0] * images[:, 0]
    for channel in range(1, CHANNELS):
        energy = energy + images[:, channel] * images[:, channel]
    current = box_filter(energy / CHANNELS) + bias_variance
    levels = [current]
    for layer_index in range(1, LAYERS):
        current = box_filter(current) + bias_variance
        levels.append(current)
    return levels

def rectified(cross, target_level, support_level):
    spread = jnp.sqrt(target_level * support_level - cross * cross)
    polar_angle = jnp.arctan2(spread, cross)
    return ((spread + (math.pi - polar_angle) * cross) / math.pi, spread, polar_angle)

def cross_forward(targets, support, target_levels, support_levels):
    inner_sum = targets[:, None, 0] * support[None, :, 0]
    for channel in range(1, CHANNELS):
        inner_sum = inner_sum + targets[:, None, channel] * support[None, :, channel]
    cross = box_filter(inner_sum / CHANNELS) + bias_variance
    saved_maps = []
    output_map = cross
    for layer_index in range(LAYERS):
        output_map, spread, polar_angle = rectified(cross, target_levels[layer_index][:, None], support_levels[layer_index][None])
        saved_maps.append((spread, polar_angle))
        if layer_index + 1 < LAYERS:
            cross = box_filter(output_map) + bias_variance
    return (lax.optimization_barrier(jnp.mean(output_map, axis=-1)), saved_maps)

def cross_backward(weight, saved_maps, targets, support, support_levels):
    upstream = weight[:, :, None]
    level_grad = None
    for layer_index in range(LAYERS - 1, -1, -1):
        spread, polar_angle = saved_maps[layer_index]
        level_term = lax.optimization_barrier(jnp.sum(upstream * spread, axis=0)) / (2.0 * math.pi * support_levels[layer_index])
        level_grad = level_term if level_grad is None else level_term + box_filter(level_grad)
        upstream = box_filter(upstream * (math.pi - polar_angle) / math.pi)
    energy_grad = box_filter(level_grad) / CHANNELS
    channel_grads = []
    for channel in range(CHANNELS):
        carried = lax.optimization_barrier(jnp.sum(upstream * targets[:, None, channel], axis=0)) / CHANNELS
        channel_grads.append(carried + 2.0 * support[:, channel] * energy_grad)
    return jnp.stack(channel_grads, axis=1)

def reference(target_pool, target_index, target_labels, dual_weights, support_images):
    targets = jnp.take(target_pool, target_index, axis=0)
    onehot = (target_labels[:, None] == jnp.arange(CLASSES)[None, :]).astype(jnp.float32)
    support_levels = self_maps(support_images)
    blocks = targets.reshape((TARGETS // TGT_DEV, TGT_DEV) + targets.shape[1:])

    def block_kernel(block):
        kernel_rows, saved_maps = cross_forward(block, support_images, self_maps(block), support_levels)
        return kernel_rows
    kernel = lax.map(block_kernel, blocks).reshape(TARGETS, SUPPORT)
    predicted = jnp.dot(kernel, dual_weights, precision=lax.Precision.HIGHEST, preferred_element_type=jnp.float32)
    residual = predicted - onehot
    weight = jnp.dot(residual, dual_weights.T, precision=lax.Precision.HIGHEST, preferred_element_type=jnp.float32)
    weight_blocks = weight.reshape(TARGETS // TGT_DEV, TGT_DEV, SUPPORT)

    def block_grad(total, pair_block):
        block, block_weight = pair_block
        kernel_rows, saved_maps = cross_forward(block, support_images, self_maps(block), support_levels)
        return (total + cross_backward(block_weight, saved_maps, block, support_images, support_levels), None)
    support_grad, unused = lax.scan(block_grad, jnp.zeros(support_images.shape, jnp.float32), (blocks, weight_blocks))
    return (residual, support_grad)
```

```python
import math

import jax
import jax.numpy as jnp
import numpy as np
from jax import lax
from jax.experimental import pallas as pl
from jax.experimental.pallas import tpu as pltpu
from jax.sharding import PartitionSpec as P

SIDE = 32
CLASSES = 100
PIXELS = 1024
BETA = 0.01
HALF = 16
TG = 64
SG = 8
AXES = ("tgt", "sup")
DIMS = (2, 4, 2, 2, 4)

ACOS = (
    1.5707962366244823,
    -0.21459087058702855,
    0.08883258279854621,
    -0.049179755946414674,
    0.02772124528589427,
    -0.011959074463765521,
    0.0025943417690760403,
)

VMEM = pl.BlockSpec(memory_space=pltpu.VMEM)
SMEM = pl.BlockSpec(memory_space=pltpu.SMEM)
F32 = jnp.float32


def pairs_of(move):
    out = []
    for src in range(int(np.prod(DIMS))):
        at = [int(v) for v in np.unravel_index(src, DIMS)]
        out.append((src, int(np.ravel_multi_index(move(*at), DIMS))))
    return out


def send(x, move):
    return lax.ppermute(x, AXES, pairs_of(move))


def even(v):
    return v ^ 1


def odd(v):
    return 3 - v


def y_move(flip):
    def move(yh, z, c, yl, x):
        y = flip(yh * 2 + yl)
        return (y // 2, z, c, y % 2, x)

    return move


STEPS = (
    lambda yh, z, c, yl, x: (yh, even(z), c, yl, x),
    lambda yh, z, c, yl, x: (yh, odd(z), c, yl, x),
    y_move(even),
    y_move(odd),
    lambda yh, z, c, yl, x: (yh, z, c, yl, even(x)),
    lambda yh, z, c, yl, x: (yh, z, c, yl, odd(x)),
)


def other_core(yh, z, c, yl, x):
    return (yh, z, 1 - c, yl, x)


def other_half(yh, z, c, yl, x):
    return (1 - yh, z, c, yl, x)


def along_z(step):
    return lambda yh, z, c, yl, x: (yh, (z + step) % 4, c, yl, x)


def box_sum(pixel_map):
    grid = pixel_map.reshape(pixel_map.shape[:-1] + (SIDE, SIDE))
    lead = [(0, 0)] * (grid.ndim - 2)
    wide = jnp.pad(grid, lead + [(0, 0), (1, 1)])
    across = wide[..., :-2] + wide[..., 1:-1] + wide[..., 2:]
    tall = jnp.pad(across, lead + [(1, 1), (0, 0)])
    return (tall[..., :-2, :] + tall[..., 1:-1, :] + tall[..., 2:, :]).reshape(pixel_map.shape)


def spread_kernel(q_ref, out_ref):
    q = q_ref[...].reshape(9 * 128, 64)
    hi = q.astype(jnp.bfloat16)
    rest = q - hi.astype(F32)
    mid = rest.astype(jnp.bfloat16)
    low = (rest - mid.astype(F32)).astype(jnp.bfloat16)
    parts = jnp.concatenate([hi.astype(F32), mid.astype(F32), low.astype(F32)], axis=1).astype(jnp.bfloat16)
    row = lax.broadcasted_iota(jnp.int32, (192, 128), 0)
    lane = lax.broadcasted_iota(jnp.int32, (192, 128), 1)
    place = (row & 63) - jnp.where(lane >= TG, SIDE, 0)

    def body(j, carry):
        pick = jnp.where(place == j, 1.0, 0.0).astype(jnp.bfloat16)
        wide = jnp.dot(parts, pick, preferred_element_type=F32)
        out_ref[:, pl.ds(j, 1)] = wide.reshape(9, 1, 128, 128)
        return carry

    lax.fori_loop(0, SIDE, body, 0)


def lanes_hi():
    return lax.broadcasted_iota(jnp.int32, (SG, 128), 1) >= TG


def down(v):
    above = jnp.where(lanes_hi(), pltpu.roll(v[HALF - 1], TG, 1), 0.0)
    below = jnp.where(lanes_hi(), 0.0, pltpu.roll(v[0], TG, 1))
    up = jnp.concatenate([above[None], v[:-1]], axis=0)
    dn = jnp.concatenate([v[1:], below[None]], axis=0)
    return v + up + dn


def target_box(v):
    col = lax.broadcasted_iota(jnp.int32, v.shape, 1)
    v = v + jnp.where(col == 0, 0.0, pltpu.roll(v, 1, 1)) + jnp.where(col == SIDE - 1, 0.0, pltpu.roll(v, SIDE - 1, 1))
    high = lax.broadcasted_iota(jnp.int32, (SIDE, 128), 1) >= TG
    above = jnp.where(high, pltpu.roll(v[HALF - 1], TG, 1), 0.0)
    below = jnp.where(high, 0.0, pltpu.roll(v[0], TG, 1))
    up = jnp.concatenate([above[None], v[:-1]], axis=0)
    dn = jnp.concatenate([v[1:], below[None]], axis=0)
    return v + up + dn


def triple(ref, j):
    return ref[pl.ds(j, 1)][0] + ref[pl.ds(j + 1, 1)][0] + ref[pl.ds(j + 2, 1)][0]


def forward_kernel(
    place_ref, x_ref, yb_ref, dual_ref,
    pred_ref, xt_ref, h0_ref, h1_ref, w0_ref, w1_ref, w2_ref, v2_ref,
    ra_ref, sa_ref, va_ref, vb_ref,
):
    energy = None
    for c in range(3):
        halves = []
        for h in range(2):
            for r in range(8):
                halves.append(x_ref[r, c * 8 : (c + 1) * 8, h * 512 : (h + 1) * 512])
        turned = jnp.concatenate(halves, axis=0).T.reshape(HALF, SIDE, 128)
        xt_ref[c] = turned
        energy = turned * turned if energy is None else energy + turned * turned
    level = target_box(energy * (1.0 / 27.0)) + BETA
    for l in range(3):
        inverse = lax.rsqrt(level)
        ra_ref[l] = inverse
        sa_ref[l] = level * inverse * (1.0 / math.pi)
        if l < 2:
            level = target_box(level * (1.0 / 9.0)) + BETA

    edge = jnp.zeros((HALF, SG, 128), F32)
    for ref in (va_ref, vb_ref, v2_ref):
        ref[0] = edge
        ref[SIDE + 1] = edge

    def wide(ref, k, j):
        return jnp.broadcast_to(ref[k, :, pl.ds(j, 1), :], (HALF, SG, 128))

    def spread(k, j):
        return yb_ref[k, pl.ds(j, 1)].reshape(HALF, SG, 128)

    def inner(j, carry):
        total = spread(0, j) * wide(xt_ref, 0, j)
        total = total + spread(1, j) * wide(xt_ref, 1, j)
        total = total + spread(2, j) * wide(xt_ref, 2, j)
        va_ref[pl.ds(j + 1, 1)] = down(total)[None]
        return carry

    lax.fori_loop(0, SIDE, inner, 0)

    def layer(l, j, from_ref):
        cross = triple(from_ref, j) + BETA
        x = cross * (spread(3 + l, j) * wide(ra_ref, l, j))
        u = jnp.abs(x) if l == 0 else x
        d = jnp.maximum(1.0 - u, 1e-30)
        s = d * lax.rsqrt(d)
        poly = jnp.full_like(u, ACOS[6] / (9.0 * math.pi))
        for k in range(5, -1, -1):
            poly = poly * u + ACOS[k] / (9.0 * math.pi)
        q = s * poly
        h = 1.0 / 9.0 - q
        if l == 0:
            h = jnp.where(x >= 0.0, h, q)
        e = 1.0 + u
        w = (spread(6 + l, j) * wide(sa_ref, l, j)) * (s * (e * lax.rsqrt(e)))
        return h, w, w + h * cross

    def layer0(j, carry):
        h, w, f = layer(0, j, va_ref)
        h0_ref[pl.ds(j, 1)] = h[None]
        w0_ref[pl.ds(j, 1)] = w[None]
        vb_ref[pl.ds(j + 1, 1)] = down(f)[None]
        return carry

    def layer1(j, carry):
        h, w, f = layer(1, j, vb_ref)
        h1_ref[pl.ds(j, 1)] = h[None]
        w1_ref[pl.ds(j, 1)] = w[None]
        va_ref[pl.ds(j + 1, 1)] = down(f)[None]
        return carry

    def layer2(j, total):
        h, w, f = layer(2, j, va_ref)
        w2_ref[pl.ds(j, 1)] = w[None]
        v2_ref[pl.ds(j + 1, 1)] = down(h)[None]
        return total + jnp.sum(f, axis=0)

    lax.fori_loop(0, SIDE, layer0, 0)
    lax.fori_loop(0, SIDE, layer1, 0)
    total = lax.fori_loop(0, SIDE, layer2, jnp.zeros((SG, 128), F32))
    kernel = total * (9.0 / PIXELS)
    both = lax.dot_general(
        kernel, dual_ref[...], (((0,), (0,)), ((), ())),
        precision=lax.Precision.HIGHEST, preferred_element_type=F32,
    )
    both = both[:TG] + both[TG:]
    for r in range(8):
        pred_ref[pl.ds(pl.multiple_of(place_ref[r] * 8, 8), 8), :] = both[r * 8 : (r + 1) * 8]


def backward_kernel(v2_ref, h1_ref, w1_ref, h0_ref, w0_ref, u_ref, l1_ref, l0_ref, va_ref, vb_ref):
    edge = jnp.zeros((HALF, SG, 128), F32)
    for ref in (va_ref, vb_ref):
        ref[0] = edge
        ref[SIDE + 1] = edge

    def layer1(j, carry):
        up = triple(v2_ref, j)
        l1_ref[pl.ds(j, 1)] = (up * w1_ref[pl.ds(j, 1)][0])[None]
        va_ref[pl.ds(j + 1, 1)] = down(up * h1_ref[pl.ds(j, 1)][0])[None]
        return carry

    def layer0(j, carry):
        up = triple(va_ref, j)
        l0_ref[pl.ds(j, 1)] = (up * w0_ref[pl.ds(j, 1)][0])[None]
        vb_ref[pl.ds(j + 1, 1)] = down(up * h0_ref[pl.ds(j, 1)][0])[None]
        return carry

    def last(j, carry):
        u_ref[pl.ds(j, 1)] = triple(vb_ref, j)[None]
        return carry

    lax.fori_loop(0, SIDE, layer1, 0)
    lax.fori_loop(0, SIDE, layer0, 0)
    lax.fori_loop(0, SIDE, last, 0)


def sum_kernel(place_ref, res_ref, dual_ref, xt_ref, u_ref, l0_ref, l1_ref, w2_ref, out_ref):
    rows = [res_ref[pl.ds(pl.multiple_of(place_ref[r] * 8, 8), 8), :] for r in range(8)]
    both = jnp.concatenate(rows + rows, axis=0)
    weight = lax.dot_general(
        dual_ref[...], both, (((1,), (1,)), ((), ())),
        precision=lax.Precision.HIGHEST, preferred_element_type=F32,
    )
    row = lax.broadcasted_iota(jnp.int32, (128, 64), 0)
    col = lax.broadcasted_iota(jnp.int32, (128, 64), 1)
    place = col - jnp.where(row >= TG, SIDE, 0)
    out_ref[...] = jnp.zeros_like(out_ref)

    def body(j, carry):
        pick = jnp.where(place == j, 1.0, 0.0).astype(jnp.bfloat16)
        up = u_ref[pl.ds(j, 1)][0] * weight[None]
        terms = [up * jnp.broadcast_to(xt_ref[c, :, pl.ds(j, 1), :], up.shape) for c in range(3)]
        terms += [ref[pl.ds(j, 1)][0] * weight[None] for ref in (l0_ref, l1_ref, w2_ref)]
        terms = jnp.stack(terms).reshape(6 * 128, 128)
        hi = terms.astype(jnp.bfloat16)
        low = (terms - hi.astype(F32)).astype(jnp.bfloat16)
        out_ref[...] += jnp.dot(hi, pick, preferred_element_type=F32) + jnp.dot(low, pick, preferred_element_type=F32)
        return carry

    lax.fori_loop(0, SIDE, body, 0)


def vm(*shape):
    return pltpu.VMEM(shape, F32)


def hb(*shape):
    return jax.ShapeDtypeStruct(shape, F32)


def params(mib):
    return pltpu.CompilerParams(vmem_limit_bytes=mib << 20)


def shards(target_pool, target_index, target_labels, dual_weights, support_images):
    tgt = lax.axis_index("tgt")
    sup = lax.axis_index("sup")
    yh, z = tgt // 8, (tgt // 2) % 4

    sibling = send(support_images, other_core)
    targets = jnp.take(target_pool, target_index - tgt * target_pool.shape[0], axis=0)
    block = targets.transpose(1, 0, 2).reshape(24, PIXELS)

    two = jnp.stack([block, send(block, other_half)])
    x_all = jnp.concatenate([two] + [send(two, along_z(k)) for k in (1, 2, 3)])
    place = jnp.stack([(yh ^ d) * 4 + (z - k) % 4 for k in range(4) for d in range(2)]).astype(jnp.int32)

    support = jnp.concatenate([support_images, sibling])
    duals = jnp.concatenate(
        [lax.dynamic_slice_in_dim(dual_weights, t * 4, 4, 0) for t in (tgt, tgt ^ 1)]
    )
    levels = [box_sum(jnp.sum(support * support, axis=1) * (1.0 / 27.0)) + BETA]
    for l in range(2):
        levels.append(box_sum(levels[-1]) * (1.0 / 9.0) + BETA)
    inverse = [lax.rsqrt(v) for v in levels]
    q = jnp.stack(
        [support[:, c] * (1.0 / 27.0) for c in range(3)]
        + inverse
        + [v * r * (1.0 / 9.0) for v, r in zip(levels, inverse)]
    )
    q = q.reshape(9, SG, 2, HALF, SIDE).transpose(0, 3, 1, 2, 4).reshape(9, 128, 64)
    yb = pl.pallas_call(
        spread_kernel, out_shape=vm(9, SIDE, 128, 128), in_specs=[VMEM], out_specs=VMEM,
        compiler_params=params(8), name="spread",
    )(q)

    column = (SIDE, HALF, SG, 128)
    padded = (SIDE + 2, HALF, SG, 128)
    flat = (3, HALF, SIDE, 128)
    pred, xt, h0, h1, w0, w1, w2, v2 = pl.pallas_call(
        forward_kernel,
        out_shape=(hb(TG, CLASSES), vm(*flat), vm(*column), vm(*column), vm(*column), vm(*column), vm(*column), vm(*padded)),
        in_specs=[SMEM, VMEM, VMEM, VMEM],
        out_specs=(VMEM,) * 8,
        scratch_shapes=[pltpu.VMEM(flat, F32), pltpu.VMEM(flat, F32), pltpu.VMEM(padded, F32), pltpu.VMEM(padded, F32)],
        compiler_params=params(14), name="forward",
    )(place, x_all, yb, duals)
    u, l1, l0 = pl.pallas_call(
        backward_kernel,
        out_shape=(vm(*column), vm(*column), vm(*column)),
        in_specs=[VMEM] * 5,
        out_specs=(VMEM,) * 3,
        scratch_shapes=[pltpu.VMEM(padded, F32), pltpu.VMEM(padded, F32)],
        compiler_params=params(10), name="backward",
    )(v2, h1, w1, h0, w0)

    own = yh * 4 + z
    at = jnp.arange(TG)
    labels = jnp.tile(target_labels, 8)
    hot = ((at // 8 == own) & (sup == 0))[:, None] & (labels[:, None] == jnp.arange(CLASSES)[None, :])
    res = pred - hot.astype(F32)
    for move in STEPS:
        res = res + send(res, move)

    sums = pl.pallas_call(
        sum_kernel, out_shape=hb(6 * 128, 64), in_specs=[SMEM] + [VMEM] * 7, out_specs=VMEM,
        compiler_params=params(8), name="weighted",
    )(place, res, duals, xt, u, l0, l1, w2)
    sums = sums.reshape(6, HALF, SG, 2, SIDE).transpose(0, 2, 3, 1, 4).reshape(6, SG, PIXELS)
    grad = None
    for l in (2, 1, 0):
        term = sums[3 + l] * 4.5 / levels[l]
        grad = term if grad is None else term + box_sum(grad) * (1.0 / 9.0)
    grad = box_sum(grad) * (1.0 / 27.0)
    full = sums[:3].transpose(1, 0, 2) * (1.0 / 3.0) + 2.0 * support * grad[:, None]
    support_grad = full[:4] + send(full[4:], other_core)
    residual = lax.dynamic_slice_in_dim(res, own * 8, 8, 0)
    return (residual, support_grad)


def solution(mesh):
    in_specs = (
        P("tgt", None, None),
        P("tgt"),
        P("tgt"),
        P("sup", None),
        P(("sup", "tgt"), None, None),
    )
    out_specs = (P("tgt", None), P(("sup", "tgt"), None, None))
    return jax.shard_map(shards, mesh=mesh, in_specs=in_specs, out_specs=out_specs, check_vma=False)
```

```python
import math

import jax
import jax.numpy as jnp
import numpy as np
from jax import lax
from jax.experimental import pallas as pl
from jax.experimental.pallas import tpu as pltpu
from jax.sharding import PartitionSpec as P

SIDE = 32
CLASSES = 100
PIXELS = 1024
BETA = 0.01
TG = 32
SG = 8
ROWS = 8
DEEP = 16
AXES = ("tgt", "sup")
DIMS = (2, 4, 2, 2, 4)

TOP = (2.4493771255467647, 0.1932864690474489, -0.013754684085600787)
BOTTOM = (2.431483473487932, 3.4797192205950016)

VMEM = pl.BlockSpec(memory_space=pltpu.VMEM)
SMEM = pl.BlockSpec(memory_space=pltpu.SMEM)
F32 = jnp.float32


def pairs_of(move):
    out = []
    for src in range(int(np.prod(DIMS))):
        at = [int(v) for v in np.unravel_index(src, DIMS)]
        out.append((src, int(np.ravel_multi_index(move(*at), DIMS))))
    return out


def send(x, move):
    return lax.ppermute(x, AXES, pairs_of(move))


def even(v):
    return v ^ 1


def odd(v):
    return 3 - v


STEPS = (
    lambda yh, z, c, yl, x: (yh, even(z), c, yl, x),
    lambda yh, z, c, yl, x: (yh, odd(z), c, yl, x),
    lambda yh, z, c, yl, x: (yh, z, c, 1 - yl, x),
    lambda yh, z, c, yl, x: (yh, z, c, yl, even(x)),
    lambda yh, z, c, yl, x: (yh, z, c, yl, odd(x)),
)


def far_z(yh, z, c, yl, x):
    return (yh, z ^ 2, c, yl, x)


OTHERS = (
    lambda yh, z, c, yl, x: (yh, z, 1 - c, yl, x),
    lambda yh, z, c, yl, x: (1 - yh, z, c, yl, x),
    lambda yh, z, c, yl, x: (1 - yh, z, 1 - c, yl, x),
)


def rows_sum(v):
    lane = lax.broadcasted_iota(jnp.int32, v.shape[1:], 1)
    above = jnp.where(lane >= TG, pltpu.roll(v[ROWS - 1], TG, 1), 0.0)
    below = jnp.where(lane < 128 - TG, pltpu.roll(v[0], 128 - TG, 1), 0.0)
    up = jnp.concatenate([above[None], v[:-1]], axis=0)
    dn = jnp.concatenate([v[1:], below[None]], axis=0)
    return v + up + dn


def down(v):
    return jnp.concatenate([rows_sum(v[:ROWS]), rows_sum(v[ROWS:])], axis=0)


def target_box(v):
    col = lax.broadcasted_iota(jnp.int32, v.shape, 1)
    v = v + jnp.where(col == 0, 0.0, pltpu.roll(v, 1, 1)) + jnp.where(col == SIDE - 1, 0.0, pltpu.roll(v, SIDE - 1, 1))
    return rows_sum(v)


def triple(ref, j):
    return ref[pl.ds(j, 1)][0] + ref[pl.ds(j + 1, 1)][0] + ref[pl.ds(j + 2, 1)][0]


def wide(ref, k, j):
    one = jnp.broadcast_to(ref[k, :, pl.ds(j, 1), :], (ROWS, SG, 128))
    return jnp.concatenate([one, one], axis=0)


def pixel_box(v):
    lane = lax.broadcasted_iota(jnp.int32, v.shape, 1)
    col = lane & (SIDE - 1)
    v = v + jnp.where(col == 0, 0.0, pltpu.roll(v, 1, 1)) + jnp.where(col == SIDE - 1, 0.0, pltpu.roll(v, PIXELS - 1, 1))
    above = jnp.where(lane < SIDE, 0.0, pltpu.roll(v, SIDE, 1))
    below = jnp.where(lane >= PIXELS - SIDE, 0.0, pltpu.roll(v, PIXELS - SIDE, 1))
    return v + above + below


def spread_kernel(s_ref, y_ref, rb_ref, sb_ref, q_ref):
    def keep(k, v):
        for i in range(ROWS):
            row = jnp.concatenate([v[:, q * 256 + i * SIDE : q * 256 + (i + 1) * SIDE] for q in range(4)], axis=1)
            for g in range(2):
                q_ref[k, (g * ROWS + i) * SG : (g * ROWS + i + 1) * SG] = row[g * SG : (g + 1) * SG]

    energy = None
    for c in range(3):
        image = s_ref[c]
        energy = image * image if energy is None else energy + image * image
        keep(c, image * (1.0 / 27.0))
    level = pixel_box(energy * (1.0 / 27.0)) + BETA
    for l in range(3):
        inverse = lax.rsqrt(level)
        keep(3 + l, inverse)
        keep(6 + l, level * inverse * (1.0 / 9.0))
        if l < 2:
            level = pixel_box(level * (1.0 / 9.0)) + BETA

    first = lax.broadcasted_iota(jnp.int32, (DEEP * SG, 128), 1) // TG * SIDE

    def body(j, carry):
        for k in range(9):
            ref = (y_ref, rb_ref, sb_ref)[k // 3]
            one = jnp.take_along_axis(q_ref[k], first + j, axis=1)
            ref[k % 3, pl.ds(j, 1)] = one.reshape(1, DEEP, SG, 128)
        return carry

    lax.fori_loop(0, SIDE, body, 0, unroll=2)


def spread(ref, k, j):
    return ref[k, pl.ds(j, 1)][0]


def forward_kernel(
    place_ref, x_ref, y_ref, rb_ref, sb_ref, dual_ref,
    pred_ref, xt_ref, h0_ref, h1_ref, w0_ref, w1_ref, w2_ref, v2_ref,
    ra_ref, sa_ref, va_ref, vb_ref,
):
    energy = None
    for c in range(3):
        parts = []
        for q in range(4):
            for r in range(4):
                parts.append(x_ref[r, c * 8 : (c + 1) * 8, q * 256 : (q + 1) * 256])
        turned = jnp.concatenate(parts, axis=0).T.reshape(ROWS, SIDE, 128)
        xt_ref[c] = turned
        energy = turned * turned if energy is None else energy + turned * turned
    level = target_box(energy * (1.0 / 27.0)) + BETA
    for l in range(3):
        inverse = lax.rsqrt(level)
        ra_ref[l] = inverse
        sa_ref[l] = level * inverse * (1.0 / math.pi)
        if l < 2:
            level = target_box(level * (1.0 / 9.0)) + BETA

    clear_edges(va_ref, vb_ref, v2_ref)

    def inner(j, carry):
        total = spread(y_ref, 0, j) * wide(xt_ref, 0, j)
        total = total + spread(y_ref, 1, j) * wide(xt_ref, 1, j)
        total = total + spread(y_ref, 2, j) * wide(xt_ref, 2, j)
        va_ref[pl.ds(j + 1, 1)] = down(total)[None]
        return carry

    lax.fori_loop(0, SIDE, inner, 0, unroll=2)

    def layer(l, j, from_ref):
        cross = triple(from_ref, j) + BETA
        x = cross * (spread(rb_ref, l, j) * wide(ra_ref, l, j))
        u = jnp.abs(x) if l == 0 else x
        d = jnp.maximum(1.0 - u * u, 1e-30)
        s = d * lax.rsqrt(d)
        top = (u * (TOP[2] / (9.0 * math.pi)) + TOP[1] / (9.0 * math.pi)) * u + TOP[0] / (9.0 * math.pi)
        q = s * (top * lax.rsqrt((u + BOTTOM[1]) * u + BOTTOM[0]))
        h = 1.0 / 9.0 - q
        if l == 0:
            h = jnp.where(x >= 0.0, h, q)
        w = (spread(sb_ref, l, j) * wide(sa_ref, l, j)) * s
        return h, w, w + h * cross

    def layer0(j, carry):
        h, w, f = layer(0, j, va_ref)
        h0_ref[pl.ds(j, 1)] = h[None]
        w0_ref[pl.ds(j, 1)] = w[None]
        vb_ref[pl.ds(j + 1, 1)] = down(f)[None]
        return carry

    def layer1(j, carry):
        h, w, f = layer(1, j, vb_ref)
        h1_ref[pl.ds(j, 1)] = h[None]
        w1_ref[pl.ds(j, 1)] = w[None]
        va_ref[pl.ds(j + 1, 1)] = down(f)[None]
        return carry

    def layer2(j, total):
        h, w, f = layer(2, j, va_ref)
        w2_ref[pl.ds(j, 1)] = w[None]
        v2_ref[pl.ds(j + 1, 1)] = down(h)[None]
        return total + jnp.sum(f.reshape(2, ROWS, SG, 128), axis=1)

    lax.fori_loop(0, SIDE, layer0, 0, unroll=4)
    lax.fori_loop(0, SIDE, layer1, 0, unroll=4)
    total = lax.fori_loop(0, SIDE, layer2, jnp.zeros((2, SG, 128), F32), unroll=4)
    kernel = total * (9.0 / PIXELS)
    wide_pred = None
    for g in range(2):
        part = lax.dot_general(
            kernel[g], dual_ref[g * SG : (g + 1) * SG], (((0,), (0,)), ((), ())),
            precision=lax.Precision.HIGHEST, preferred_element_type=F32,
        )
        wide_pred = part if wide_pred is None else wide_pred + part
    pred = wide_pred[:32] + wide_pred[32:64] + wide_pred[64:96] + wide_pred[96:]
    for r in range(4):
        pred_ref[pl.ds(pl.multiple_of(place_ref[r] * 8, 8), 8), :] = pred[r * 8 : (r + 1) * 8]


def clear_edges(*refs):
    for ref in refs:
        ref[0] = jnp.zeros((DEEP, SG, 128), F32)
        ref[SIDE + 1] = jnp.zeros((DEEP, SG, 128), F32)


def at(ref, j):
    return ref[pl.ds(j, 1)][0]


def back_kernel_a(v2_ref, h1_ref, w1_ref, w2_ref, rb_ref, l1_ref, v1_ref, p2_ref):
    clear_edges(v1_ref, p2_ref)

    def body(j, carry):
        up = triple(v2_ref, j)
        rb = spread(rb_ref, 1, j)
        l1_ref[pl.ds(j, 1)] = (up * at(w1_ref, j) * (rb * rb))[None]
        v1_ref[pl.ds(j + 1, 1)] = down(up * at(h1_ref, j))[None]
        rb = spread(rb_ref, 2, j)
        p2_ref[pl.ds(j + 1, 1)] = down(at(w2_ref, j) * (rb * rb))[None]
        return carry

    lax.fori_loop(0, SIDE, body, 0, unroll=4)


def back_kernel_b(v1_ref, h0_ref, w0_ref, l1_ref, p2_ref, rb_ref, l0_ref, v0_ref, p1_ref):
    clear_edges(v0_ref, p1_ref)

    def body(j, carry):
        up = triple(v1_ref, j)
        rb = spread(rb_ref, 0, j)
        l0_ref[pl.ds(j, 1)] = (up * at(w0_ref, j) * (rb * rb))[None]
        v0_ref[pl.ds(j + 1, 1)] = down(up * at(h0_ref, j))[None]
        p1_ref[pl.ds(j + 1, 1)] = down(at(l1_ref, j) + triple(p2_ref, j) * (1.0 / 9.0))[None]
        return carry

    lax.fori_loop(0, SIDE, body, 0, unroll=4)


def back_kernel_c(l0_ref, p1_ref, p0_ref):
    clear_edges(p0_ref)

    def body(j, carry):
        p0_ref[pl.ds(j + 1, 1)] = down(at(l0_ref, j) + triple(p1_ref, j) * (1.0 / 9.0))[None]
        return carry

    lax.fori_loop(0, SIDE, body, 0, unroll=4)


def back_kernel_d(v0_ref, p0_ref, up_ref, energy_ref):
    def body(j, carry):
        up_ref[pl.ds(j, 1)] = triple(v0_ref, j)[None]
        energy_ref[pl.ds(j, 1)] = (triple(p0_ref, j) * 27.0)[None]
        return carry

    lax.fori_loop(0, SIDE, body, 0, unroll=4)


def back_kernel_e(up_ref, energy_ref, xt_ref, y_ref, g_ref):
    def body(j, carry):
        up, energy = at(up_ref, j), at(energy_ref, j)
        for c in range(3):
            g_ref[c, pl.ds(j, 1)] = (up * wide(xt_ref, c, j) + energy * spread(y_ref, c, j))[None]
        return carry

    lax.fori_loop(0, SIDE, body, 0, unroll=2)


def fold(a, b, step):
    lane = lax.broadcasted_iota(jnp.int32, a.shape, 1)
    return jnp.where((lane & step) == 0, a + pltpu.roll(a, 128 - step, 1), b + pltpu.roll(b, step, 1))


def sum_kernel(place_ref, res_ref, dual_ref, g_ref, own_ref, *out_refs):
    own_ref[...] = res_ref[pl.ds(pl.multiple_of(place_ref[0] * 8, 8), 8), :]
    rows = [res_ref[pl.ds(pl.multiple_of(place_ref[r] * 8, 8), 8), :] for r in range(4)]
    weight = lax.dot_general(
        dual_ref[...] * (1.0 / 3.0), jnp.concatenate(rows * 4, axis=0), (((1,), (1,)), ((), ())),
        precision=lax.Precision.HIGHEST, preferred_element_type=F32,
    )
    weight = jnp.broadcast_to(weight.reshape(2, 1, SG, 128), (2, ROWS, SG, 128)).reshape(DEEP, SG, 128)
    row = lax.broadcasted_iota(jnp.int32, (512, 128), 0)
    col = lax.broadcasted_iota(jnp.int32, (512, 128), 1)
    place = col - (row & 127) // TG * SIDE - (row & 31) // 8 - lax.shift_right_logical(row, 7) * 4
    total = jnp.zeros((3 * 128, 128), F32)
    for j in range(0, SIDE, 16):
        pick = jnp.where(place == j, 1.0, 0.0).astype(jnp.bfloat16)
        his, lows = [], []
        for k in range(j, j + 16, 4):
            four = [(g_ref[:, k + n] * weight).reshape(3 * 128, 128) for n in range(4)]
            term = fold(fold(four[0], four[2], 16), fold(four[1], four[3], 16), 8)
            hi = term.astype(jnp.bfloat16)
            his.append(hi)
            lows.append((term - hi.astype(F32)).astype(jnp.bfloat16))
        total = total + jnp.dot(jnp.concatenate(his, axis=1), pick, preferred_element_type=F32)
        total = total + jnp.dot(jnp.concatenate(lows, axis=1), pick, preferred_element_type=F32)
    for c in range(3):
        for g in range(2):
            image = [total[((c * 2 + g) * ROWS + i) * SG : ((c * 2 + g) * ROWS + i + 1) * SG] for i in range(ROWS)]
            line = jnp.concatenate([image[i][:, q * SIDE : (q + 1) * SIDE] for q in range(4) for i in range(ROWS)], axis=1)
            out_refs[2 * g][c] = line[:4]
            out_refs[2 * g + 1][c] = line[4:]


def near(x):
    return pltpu.with_memory_space_constraint(x, pltpu.VMEM)


def vm(*shape):
    return pltpu.VMEM(shape, F32)


def hb(*shape):
    return jax.ShapeDtypeStruct(shape, F32)


def params(mib):
    return pltpu.CompilerParams(vmem_limit_bytes=mib << 20)


def shards(target_pool, target_index, target_labels, dual_weights, support_images):
    tgt = lax.axis_index("tgt")
    sup = lax.axis_index("sup")
    z = (tgt // 2) % 4

    mine = support_images.transpose(1, 0, 2)
    near_images = send(mine, OTHERS[0])
    others = [near_images, send(mine, OTHERS[1]), send(mine, OTHERS[2])]
    target_index, near_images = lax.optimization_barrier((target_index, near_images))
    support = jnp.concatenate([mine] + others, axis=1)
    targets = target_pool.at[target_index - tgt * target_pool.shape[0]].get(mode="promise_in_bounds")
    block = targets.transpose(1, 0, 2).reshape(24, PIXELS)
    x_all = jnp.stack([block, send(block, STEPS[0]), send(block, STEPS[1]), send(block, far_z)])
    place = jnp.stack([z, z ^ 1, 3 - z, z ^ 2]).astype(jnp.int32)

    duals = jnp.concatenate(
        [lax.dynamic_slice_in_dim(dual_weights, (tgt ^ k) * 4, 4, 0) for k in (0, 1, 8, 9)]
    )
    spread_shape = (3, SIDE, DEEP, SG, 128)
    y_wide, rb_wide, sb_wide = pl.pallas_call(
        spread_kernel, out_shape=(vm(*spread_shape),) * 3, in_specs=[VMEM], out_specs=(VMEM,) * 3,
        scratch_shapes=[pltpu.VMEM((9, DEEP * SG, 128), F32)], compiler_params=params(6), name="spread",
    )(support)

    column = (SIDE, DEEP, SG, 128)
    padded = (SIDE + 2, DEEP, SG, 128)
    flat = (3, ROWS, SIDE, 128)

    def near_call(kernel, outs, ins, name, scratch=(), mib=6):
        return pl.pallas_call(
            kernel, out_shape=tuple(vm(*o) for o in outs), in_specs=[VMEM] * len(ins), out_specs=(VMEM,) * len(outs),
            scratch_shapes=[pltpu.VMEM(v, F32) for v in scratch], compiler_params=params(mib), name=name,
        )(*map(near, ins))

    pred, xt, h0, h1, w0, w1, w2, v2 = pl.pallas_call(
        forward_kernel,
        out_shape=(hb(TG, CLASSES), vm(*flat), vm(*column), vm(*column), vm(*column), vm(*column), vm(*column), vm(*padded)),
        in_specs=[SMEM] + [VMEM] * 5,
        out_specs=(VMEM,) * 8,
        scratch_shapes=[pltpu.VMEM(flat, F32), pltpu.VMEM(flat, F32), pltpu.VMEM(padded, F32), pltpu.VMEM(padded, F32)],
        compiler_params=params(14), name="forward",
    )(place, x_all, near(y_wide), near(rb_wide), near(sb_wide), duals)

    labels = jnp.tile(target_labels, 4)
    hot = ((jnp.arange(TG) // 8 == z) & (sup == 0))[:, None] & (labels[:, None] == jnp.arange(CLASSES)[None, :])
    res = pred - hot.astype(F32)

    res, v2 = lax.optimization_barrier((res, v2))
    new = send(res, STEPS[0])
    l1, v1, p2 = near_call(back_kernel_a, (column, padded, padded), (v2, h1, w1, w2, rb_wide), "back_a")
    res, v1 = lax.optimization_barrier((res + new, v1))
    new = send(res, STEPS[1])
    l0, v0, p1 = near_call(back_kernel_b, (column, padded, padded), (v1, h0, w0, l1, p2, rb_wide), "back_b")
    res, l0 = lax.optimization_barrier((res + new, l0))
    new = send(res, STEPS[2])
    (p0,) = near_call(back_kernel_c, (padded,), (l0, p1), "back_c")
    res, p0 = lax.optimization_barrier((res + new, p0))
    new = send(res, STEPS[3])
    up, energy = near_call(back_kernel_d, (column, column), (v0, p0), "back_d")
    res, up = lax.optimization_barrier((res + new, up))
    new = send(res, STEPS[4])
    (g,) = near_call(back_kernel_e, ((3,) + column,), (up, energy, xt, y_wide), "back_e")
    res = res + new

    residual, *parts = pl.pallas_call(
        sum_kernel, out_shape=(hb(8, CLASSES),) + (hb(3, 4, PIXELS),) * 4,
        in_specs=[SMEM] + [VMEM] * 3, out_specs=(VMEM,) * 5,
        compiler_params=params(10), name="weighted",
    )(place, res, duals, near(g))
    far1, far2 = send(parts[2], OTHERS[1]), send(parts[3], OTHERS[2])
    total = parts[0] + send(parts[1], OTHERS[0]) + far1 + far2
    return (residual, total.transpose(1, 0, 2))


def solution(mesh):
    in_specs = (
        P("tgt", None, None),
        P("tgt"),
        P("tgt"),
        P("sup", None),
        P(("sup", "tgt"), None, None),
    )
    out_specs = (P("tgt", None), P(("sup", "tgt"), None, None))
    return jax.shard_map(shards, mesh=mesh, in_specs=in_specs, out_specs=out_specs, check_vma=False)
```

```python
import math

import jax
import jax.numpy as jnp
import numpy as np
from jax import lax
from jax.experimental import pallas as pl
from jax.experimental.pallas import tpu as pltpu
from jax.sharding import PartitionSpec as P

SIDE = 32
CLASSES = 100
PIXELS = 1024
BETA = 0.01
TG = 32
SG = 8
ROWS = 8
DEEP = 16
AXES = ("tgt", "sup")
DIMS = (2, 4, 2, 2, 4)

TOP = (2.4493771255467647, 0.1932864690474489, -0.013754684085600787)
BOTTOM = (2.431483473487932, 3.4797192205950016)

VMEM = pl.BlockSpec(memory_space=pltpu.VMEM)
SMEM = pl.BlockSpec(memory_space=pltpu.SMEM)
F32 = jnp.float32


def pairs_of(move):
    out = []
    for src in range(int(np.prod(DIMS))):
        at = [int(v) for v in np.unravel_index(src, DIMS)]
        out.append((src, int(np.ravel_multi_index(move(*at), DIMS))))
    return out


def send(x, move):
    return lax.ppermute(x, AXES, pairs_of(move))


def even(v):
    return v ^ 1


def odd(v):
    return 3 - v


STEPS = (
    lambda yh, z, c, yl, x: (yh, even(z), c, yl, x),
    lambda yh, z, c, yl, x: (yh, odd(z), c, yl, x),
    lambda yh, z, c, yl, x: (yh, z, c, 1 - yl, x),
    lambda yh, z, c, yl, x: (yh, z, c, yl, even(x)),
    lambda yh, z, c, yl, x: (yh, z, c, yl, odd(x)),
)


def far_z(yh, z, c, yl, x):
    return (yh, z ^ 2, c, yl, x)


def far_x(yh, z, c, yl, x):
    return (yh, z, c, yl, x ^ 2)


def other_core(yh, z, c, yl, x):
    return (yh, z, 1 - c, yl, x)


def other_y(yh, z, c, yl, x):
    return (1 - yh, z, c, yl, x)


def rows_sum(v):
    lane = lax.broadcasted_iota(jnp.int32, v.shape[1:], 1)
    above = jnp.where(lane >= TG, pltpu.roll(v[ROWS - 1], TG, 1), 0.0)
    below = jnp.where(lane < 128 - TG, pltpu.roll(v[0], 128 - TG, 1), 0.0)
    line = [above] + [v[i] for i in range(ROWS)] + [below]
    out = []
    for i in range(1, ROWS + 1, 2):
        both = line[i] + line[i + 1]
        out += [line[i - 1] + both, both + line[i + 2]]
    return jnp.stack(out)


def down(v):
    return jnp.concatenate([rows_sum(v[:ROWS]), rows_sum(v[ROWS:])], axis=0)


def target_box(v):
    col = lax.broadcasted_iota(jnp.int32, v.shape, 1)
    v = v + jnp.where(col == 0, 0.0, pltpu.roll(v, 1, 1)) + jnp.where(col == SIDE - 1, 0.0, pltpu.roll(v, SIDE - 1, 1))
    return rows_sum(v)


def columns(ref, k):
    first, left, right, last = [ref[pl.ds(2 * k + n, 1)][0] for n in range(4)]
    both = left + right
    return ((2 * k, first + both), (2 * k + 1, both + last))


def wide(ref, k, j):
    one = jnp.broadcast_to(ref[k, :, pl.ds(j, 1), :], (ROWS, SG, 128))
    return jnp.concatenate([one, one], axis=0)


def pixel_box(v):
    lane = lax.broadcasted_iota(jnp.int32, v.shape, 1)
    col = lane & (SIDE - 1)
    v = v + jnp.where(col == 0, 0.0, pltpu.roll(v, 1, 1)) + jnp.where(col == SIDE - 1, 0.0, pltpu.roll(v, PIXELS - 1, 1))
    above = jnp.where(lane < SIDE, 0.0, pltpu.roll(v, SIDE, 1))
    below = jnp.where(lane >= PIXELS - SIDE, 0.0, pltpu.roll(v, PIXELS - SIDE, 1))
    return v + above + below


def spread_kernel(s_ref, y_ref, rb_ref, sb_ref, q_ref):
    def keep(k, v):
        for i in range(ROWS):
            row = jnp.concatenate([v[:, q * 256 + i * SIDE : q * 256 + (i + 1) * SIDE] for q in range(4)], axis=1)
            for g in range(2):
                q_ref[k, (g * ROWS + i) * SG : (g * ROWS + i + 1) * SG] = row[g * SG : (g + 1) * SG]

    energy = None
    for c in range(3):
        image = s_ref[c]
        energy = image * image if energy is None else energy + image * image
        keep(c, image * (1.0 / 27.0))
    level = pixel_box(energy * (1.0 / 27.0)) + BETA
    for l in range(3):
        inverse = lax.rsqrt(level)
        keep(3 + l, inverse)
        if l < 2:
            level = pixel_box(level * (1.0 / 9.0)) + BETA

    first = lax.broadcasted_iota(jnp.int32, (DEEP * SG, 128), 1) // TG * SIDE

    def body(j, carry):
        for k in range(6):
            one = jnp.take_along_axis(q_ref[k], first + j, axis=1).reshape(1, DEEP, SG, 128)
            if k < 3:
                y_ref[k, pl.ds(j, 1)] = one
            else:
                rb_ref[k - 3, pl.ds(j, 1)] = one
                sb_ref[k - 3, pl.ds(j, 1)] = lax.rsqrt(one * one) * (1.0 / 9.0)
        return carry

    lax.fori_loop(0, SIDE, body, 0, unroll=2)


def spread(ref, k, j):
    return ref[k, pl.ds(j, 1)][0]


def own_duals(place_ref, dual_ref):
    return [dual_ref[pl.ds(place_ref[4 + k] * 4, 4), :] for k in range(4)]


def forward_kernel(
    place_ref, x_ref, y_ref, rb_ref, sb_ref, dual_ref, label_ref,
    pred_ref, xt_ref, h0_ref, h1_ref, w0_ref, w1_ref, w2_ref, v2_ref,
    ra_ref, sa_ref, va_ref, vb_ref,
):
    energy = None
    for c in range(3):
        parts = []
        for q in range(4):
            for r in range(4):
                parts.append(x_ref[r, c * 8 : (c + 1) * 8, q * 256 : (q + 1) * 256])
        turned = jnp.concatenate(parts, axis=0).T.reshape(ROWS, SIDE, 128)
        xt_ref[c] = turned
        energy = turned * turned if energy is None else energy + turned * turned
    level = target_box(energy * (1.0 / 27.0)) + BETA
    for l in range(3):
        inverse = lax.rsqrt(level)
        ra_ref[l] = inverse
        sa_ref[l] = level * inverse * (1.0 / math.pi)
        if l < 2:
            level = target_box(level * (1.0 / 9.0)) + BETA

    clear_edges(va_ref, vb_ref, v2_ref)

    def inner(j, carry):
        total = spread(y_ref, 0, j) * wide(xt_ref, 0, j)
        total = total + spread(y_ref, 1, j) * wide(xt_ref, 1, j)
        total = total + spread(y_ref, 2, j) * wide(xt_ref, 2, j)
        va_ref[pl.ds(j + 1, 1)] = down(total)[None]
        return carry

    lax.fori_loop(0, SIDE, inner, 0, unroll=2)

    def layer(l, j, around):
        cross = around + BETA
        x = cross * (spread(rb_ref, l, j) * wide(ra_ref, l, j))
        u = jnp.abs(x) if l == 0 else x
        d = jnp.maximum(1.0 - u * u, 1e-30)
        s = d * lax.rsqrt(d)
        top = (u * (TOP[2] / (9.0 * math.pi)) + TOP[1] / (9.0 * math.pi)) * u + TOP[0] / (9.0 * math.pi)
        q = s * (top * lax.rsqrt((u + BOTTOM[1]) * u + BOTTOM[0]))
        h = 1.0 / 9.0 - q
        if l == 0:
            h = jnp.where(x >= 0.0, h, q)
        w = (spread(sb_ref, l, j) * wide(sa_ref, l, j)) * s
        return h, w, w + h * cross

    def layer0(k, carry):
        for j, around in columns(va_ref, k):
            h, w, f = layer(0, j, around)
            h0_ref[pl.ds(j, 1)] = h[None]
            w0_ref[pl.ds(j, 1)] = w[None]
            vb_ref[pl.ds(j + 1, 1)] = down(f)[None]
        return carry

    def layer1(k, carry):
        for j, around in columns(vb_ref, k):
            h, w, f = layer(1, j, around)
            h1_ref[pl.ds(j, 1)] = h[None]
            w1_ref[pl.ds(j, 1)] = w[None]
            va_ref[pl.ds(j + 1, 1)] = down(f)[None]
        return carry

    def layer2(k, total):
        for j, around in columns(va_ref, k):
            h, w, f = layer(2, j, around)
            w2_ref[pl.ds(j, 1)] = w[None]
            v2_ref[pl.ds(j + 1, 1)] = down(h)[None]
            total = total + jnp.sum(f.reshape(2, ROWS, SG, 128), axis=1)
        return total

    lax.fori_loop(0, SIDE // 2, layer0, 0, unroll=2)
    lax.fori_loop(0, SIDE // 2, layer1, 0, unroll=2)
    total = lax.fori_loop(0, SIDE // 2, layer2, jnp.zeros((2, SG, 128), F32), unroll=2)
    kernel = total * (9.0 / PIXELS)
    duals = own_duals(place_ref, dual_ref)
    wide_pred = None
    for g in range(2):
        part = lax.dot_general(
            kernel[g], jnp.concatenate(duals[2 * g : 2 * g + 2], axis=0), (((0,), (0,)), ((), ())),
            precision=lax.Precision.HIGHEST, preferred_element_type=F32,
        )
        wide_pred = part if wide_pred is None else wide_pred + part
    pred = wide_pred[:32] + wide_pred[32:64] + wide_pred[64:96] + wide_pred[96:]
    for r in range(4):
        rows = pred[r * 8 : (r + 1) * 8]
        if r == 0:
            row = lax.broadcasted_iota(jnp.int32, rows.shape, 0)
            own = jnp.zeros(rows.shape, jnp.int32)
            for t in range(8):
                own = jnp.where(row == t, label_ref[t], own)
            hot = (own == lax.broadcasted_iota(jnp.int32, rows.shape, 1)) & (place_ref[8] == 0)
            rows = rows - jnp.where(hot, 1.0, 0.0)
        pred_ref[pl.ds(pl.multiple_of(place_ref[r] * 8, 8), 8), :] = rows


def clear_edges(*refs):
    for ref in refs:
        ref[0] = jnp.zeros((DEEP, SG, 128), F32)
        ref[SIDE + 1] = jnp.zeros((DEEP, SG, 128), F32)


def at(ref, j):
    return ref[pl.ds(j, 1)][0]


def back_kernel_a(v2_ref, h1_ref, w1_ref, w2_ref, h0_ref, w0_ref, rb_ref, v0_ref, l0_ref, p1_ref, l1_ref, v1_ref, p2_ref):
    clear_edges(v1_ref, p2_ref, v0_ref, p1_ref)

    def layer1(k, carry):
        for j, up in columns(v2_ref, k):
            rb = spread(rb_ref, 1, j)
            l1_ref[pl.ds(j, 1)] = (up * at(w1_ref, j) * (rb * rb))[None]
            v1_ref[pl.ds(j + 1, 1)] = down(up * at(h1_ref, j))[None]
            rb = spread(rb_ref, 2, j)
            p2_ref[pl.ds(j + 1, 1)] = down(at(w2_ref, j) * (rb * rb))[None]
        return carry

    def layer0(k, carry):
        for (j, up), (_, sums) in zip(columns(v1_ref, k), columns(p2_ref, k)):
            rb = spread(rb_ref, 0, j)
            l0_ref[pl.ds(j, 1)] = (up * at(w0_ref, j) * (rb * rb))[None]
            v0_ref[pl.ds(j + 1, 1)] = down(up * at(h0_ref, j))[None]
            p1_ref[pl.ds(j + 1, 1)] = down(at(l1_ref, j) + sums * (1.0 / 9.0))[None]
        return carry

    lax.fori_loop(0, SIDE // 2, layer1, 0, unroll=2)
    lax.fori_loop(0, SIDE // 2, layer0, 0, unroll=2)


def back_kernel_b(l0_ref, p1_ref, p0_ref):
    clear_edges(p0_ref)

    def body(k, carry):
        for j, sums in columns(p1_ref, k):
            p0_ref[pl.ds(j + 1, 1)] = down(at(l0_ref, j) + sums * (1.0 / 9.0))[None]
        return carry

    lax.fori_loop(0, SIDE // 2, body, 0, unroll=2)


def back_kernel_c(v0_ref, p0_ref, xt_ref, y_ref, g_ref):
    def body(k, carry):
        for (j, up), (_, energy) in zip(columns(v0_ref, k), columns(p0_ref, k)):
            energy = energy * 27.0
            for c in range(3):
                g_ref[c, pl.ds(j, 1)] = (up * wide(xt_ref, c, j) + energy * spread(y_ref, c, j))[None]
        return carry

    lax.fori_loop(0, SIDE // 2, body, 0)


def sum_kernel(place_ref, res_ref, dual_ref, g_ref, own_ref, *out_refs):
    own_ref[...] = res_ref[pl.ds(pl.multiple_of(place_ref[0] * 8, 8), 8), :]
    rows = [res_ref[pl.ds(pl.multiple_of(place_ref[r] * 8, 8), 8), :] for r in range(4)]
    weight = lax.dot_general(
        jnp.concatenate(own_duals(place_ref, dual_ref), axis=0) * (1.0 / 3.0), jnp.concatenate(rows * 4, axis=0), (((1,), (1,)), ((), ())),
        precision=lax.Precision.HIGHEST, preferred_element_type=F32,
    )
    weight = jnp.broadcast_to(weight.reshape(2, 1, SG, 128), (2, ROWS, SG, 128)).reshape(DEEP, SG, 128)
    row = lax.broadcasted_iota(jnp.int32, (512, 128), 0)
    col = lax.broadcasted_iota(jnp.int32, (512, 128), 1)
    place = col - (row & 127) // TG * SIDE - lax.shift_right_logical(row, 7)
    total = jnp.zeros((3 * 128, 128), F32)
    for j in range(0, SIDE, 4):
        pick = jnp.where(place == j, 1.0, 0.0).astype(jnp.bfloat16)
        his, lows = [], []
        for k in range(4):
            term = (g_ref[:, j + k] * weight).reshape(3 * 128, 128)
            hi = term.astype(jnp.bfloat16)
            his.append(hi)
            lows.append((term - hi.astype(F32)).astype(jnp.bfloat16))
        total = total + jnp.dot(jnp.concatenate(his, axis=1), pick, preferred_element_type=F32)
        total = total + jnp.dot(jnp.concatenate(lows, axis=1), pick, preferred_element_type=F32)
    for c in range(3):
        for g in range(2):
            image = [total[((c * 2 + g) * ROWS + i) * SG : ((c * 2 + g) * ROWS + i + 1) * SG] for i in range(ROWS)]
            line = jnp.concatenate([image[i][:, q * SIDE : (q + 1) * SIDE] for q in range(4) for i in range(ROWS)], axis=1)
            out_refs[0][c, g * 4 : g * 4 + 4] = line[:4]
            out_refs[1][c, g * 4 : g * 4 + 4] = line[4:]


def near(x):
    return pltpu.with_memory_space_constraint(x, pltpu.VMEM)


def vm(*shape):
    return pltpu.VMEM(shape, F32)


def hb(*shape):
    return jax.ShapeDtypeStruct(shape, F32)


def params(mib):
    return pltpu.CompilerParams(vmem_limit_bytes=mib << 20)


def shards(target_pool, target_index, target_labels, dual_weights, support_images):
    tgt = lax.axis_index("tgt")
    sup = lax.axis_index("sup")
    z = (tgt // 2) % 4

    mine = support_images.transpose(1, 0, 2)
    pair = jnp.concatenate([mine, send(mine, other_core)], axis=1)
    target_index, pair = lax.optimization_barrier((target_index, pair))
    support = jnp.concatenate([pair, send(pair, other_y)], axis=1)
    rows = (target_index - tgt * target_pool.shape[0]).astype(jnp.uint32)
    targets = target_pool.at[rows].get(mode="promise_in_bounds")
    block = targets.transpose(1, 0, 2).reshape(24, PIXELS)
    x_all = jnp.stack([block, send(block, STEPS[0]), send(block, STEPS[1]), send(block, far_z)])
    place = jnp.stack([z, z ^ 1, 3 - z, z ^ 2] + [tgt ^ k for k in (0, 1, 8, 9)] + [sup]).astype(jnp.int32)

    spread_shape = (3, SIDE, DEEP, SG, 128)
    y_wide, rb_wide, sb_wide = pl.pallas_call(
        spread_kernel, out_shape=(vm(*spread_shape),) * 3, in_specs=[VMEM], out_specs=(VMEM,) * 3,
        scratch_shapes=[pltpu.VMEM((6, DEEP * SG, 128), F32)], compiler_params=params(6), name="spread",
    )(support)

    column = (SIDE, DEEP, SG, 128)
    padded = (SIDE + 2, DEEP, SG, 128)
    flat = (3, ROWS, SIDE, 128)

    def near_call(kernel, outs, ins, name, scratch=(), mib=6):
        return pl.pallas_call(
            kernel, out_shape=tuple(vm(*o) for o in outs), in_specs=[VMEM] * len(ins), out_specs=(VMEM,) * len(outs),
            scratch_shapes=[pltpu.VMEM(v, F32) for v in scratch], compiler_params=params(mib), name=name,
        )(*map(near, ins))

    pred, xt, h0, h1, w0, w1, w2, v2 = pl.pallas_call(
        forward_kernel,
        out_shape=(hb(TG, CLASSES), vm(*flat), vm(*column), vm(*column), vm(*column), vm(*column), vm(*column), vm(*padded)),
        in_specs=[SMEM] + [VMEM] * 5 + [SMEM],
        out_specs=(VMEM,) * 8,
        scratch_shapes=[pltpu.VMEM(flat, F32), pltpu.VMEM(flat, F32), pltpu.VMEM(padded, F32), pltpu.VMEM(padded, F32)],
        compiler_params=params(14), name="forward",
    )(place, x_all, near(y_wide), near(rb_wide), near(sb_wide), dual_weights, target_labels)

    def around(res, moves):
        near_a, near_b, far = [send(res, move) for move in moves]
        return lambda: (res + near_a) + (near_b + far)

    res, v2 = lax.optimization_barrier((pred, v2))
    added = around(res, (STEPS[0], STEPS[1], far_z))
    v0, l0, p1 = near_call(
        back_kernel_a, (padded, column, padded), (v2, h1, w1, w2, h0, w0, rb_wide), "back_a",
        scratch=(column, padded, padded), mib=9,
    )
    res, l0 = lax.optimization_barrier((added(), l0))
    new = send(res, STEPS[2])
    (p0,) = near_call(back_kernel_b, (padded,), (l0, p1), "back_b")
    res, p0 = lax.optimization_barrier((res + new, p0))
    added = around(res, (STEPS[3], STEPS[4], far_x))
    (g,) = near_call(back_kernel_c, ((3,) + column,), (v0, p0, xt, y_wide), "back_c")
    res = added()

    residual, *parts = pl.pallas_call(
        sum_kernel, out_shape=(hb(8, CLASSES),) + (hb(3, 8, PIXELS),) * 2,
        in_specs=[SMEM] + [VMEM] * 3, out_specs=(VMEM,) * 3,
        compiler_params=params(10), name="weighted",
    )(place, res, dual_weights, near(g))
    pair = parts[0] + send(parts[1], other_core)
    total = pair[:, :4] + send(pair[:, 4:], other_y)
    return (residual, total.transpose(1, 0, 2))


def solution(mesh):
    in_specs = (
        P("tgt", None, None),
        P("tgt"),
        P("tgt"),
        P("sup", None),
        P(("sup", "tgt"), None, None),
    )
    out_specs = (P("tgt", None), P(("sup", "tgt"), None, None))
    return jax.shard_map(shards, mesh=mesh, in_specs=in_specs, out_specs=out_specs, check_vma=False)
```

```python
import math

import jax
import jax.numpy as jnp
import numpy as np
from jax import lax
from jax.experimental import pallas as pl
from jax.experimental.pallas import tpu as pltpu
from jax.sharding import PartitionSpec as P

SIDE = 32
CLASSES = 100
PIXELS = 1024
BETA = 0.01
TG = 32
SG = 8
ROWS = 8
DEEP = 16
AXES = ("tgt", "sup")
DIMS = (2, 4, 2, 2, 4)

TOP = (2.4493771255467647, 0.1932864690474489, -0.013754684085600787)
BOTTOM = (2.431483473487932, 3.4797192205950016)

VMEM = pl.BlockSpec(memory_space=pltpu.VMEM)
SMEM = pl.BlockSpec(memory_space=pltpu.SMEM)
F32 = jnp.float32


def pairs_of(move):
    out = []
    for src in range(int(np.prod(DIMS))):
        at = [int(v) for v in np.unravel_index(src, DIMS)]
        out.append((src, int(np.ravel_multi_index(move(*at), DIMS))))
    return out


def send(x, move):
    return lax.ppermute(x, AXES, pairs_of(move))


def even(v):
    return v ^ 1


def odd(v):
    return 3 - v


STEPS = (
    lambda yh, z, c, yl, x: (yh, even(z), c, yl, x),
    lambda yh, z, c, yl, x: (yh, odd(z), c, yl, x),
    lambda yh, z, c, yl, x: (yh, z, c, 1 - yl, x),
    lambda yh, z, c, yl, x: (yh, z, c, yl, even(x)),
    lambda yh, z, c, yl, x: (yh, z, c, yl, odd(x)),
)


def far_z(yh, z, c, yl, x):
    return (yh, z ^ 2, c, yl, x)


def far_x(yh, z, c, yl, x):
    return (yh, z, c, yl, x ^ 2)


def other_core(yh, z, c, yl, x):
    return (yh, z, 1 - c, yl, x)


def other_y(yh, z, c, yl, x):
    return (1 - yh, z, c, yl, x)


def rows_sum(v):
    lane = lax.broadcasted_iota(jnp.int32, v.shape[1:], 1)
    above = jnp.where(lane >= TG, pltpu.roll(v[ROWS - 1], TG, 1), 0.0)
    below = jnp.where(lane < 128 - TG, pltpu.roll(v[0], 128 - TG, 1), 0.0)
    line = [above] + [v[i] for i in range(ROWS)] + [below]
    out = []
    for i in range(1, ROWS + 1, 2):
        both = line[i] + line[i + 1]
        out += [line[i - 1] + both, both + line[i + 2]]
    return jnp.stack(out)


def down(v):
    return jnp.concatenate([rows_sum(v[:ROWS]), rows_sum(v[ROWS:])], axis=0)


def target_box(v):
    col = lax.broadcasted_iota(jnp.int32, v.shape, 1)
    v = v + jnp.where(col == 0, 0.0, pltpu.roll(v, 1, 1)) + jnp.where(col == SIDE - 1, 0.0, pltpu.roll(v, SIDE - 1, 1))
    return rows_sum(v)


def columns(ref, k):
    first, left, right, last = [ref[pl.ds(2 * k + n, 1)][0] for n in range(4)]
    both = left + right
    return ((2 * k, first + both), (2 * k + 1, both + last))


def wide(ref, k, j):
    one = jnp.broadcast_to(ref[k, :, pl.ds(j, 1), :], (ROWS, SG, 128))
    return jnp.concatenate([one, one], axis=0)


def pick_kernel(
    index_hbm, label_hbm, pool_hbm, dual_hbm, mine_hbm, block_ref, dual_ref, mine_ref, hot_ref,
    index_ref, label_ref, pool_ref, index_sem, label_sem, pool_sem, dual_sem, mine_sem,
):
    copies = [
        pltpu.make_async_copy(index_hbm, index_ref, index_sem),
        pltpu.make_async_copy(pool_hbm, pool_ref, pool_sem),
        pltpu.make_async_copy(label_hbm, label_ref, label_sem),
        pltpu.make_async_copy(dual_hbm, dual_ref, dual_sem),
        pltpu.make_async_copy(mine_hbm, mine_ref, mine_sem),
    ]
    for copy in copies:
        copy.start()
    for copy in copies:
        copy.wait()
    base = lax.axis_index("tgt") * pool_ref.shape[1]
    for t in range(8):
        one = pool_ref[:, pl.ds(index_ref[t] - base, 1), :]
        for c in range(3):
            block_ref[c * 8 + t : c * 8 + t + 1] = one[c]
    row = lax.broadcasted_iota(jnp.int32, (8, CLASSES), 0)
    own = jnp.zeros((8, CLASSES), jnp.int32)
    for t in range(8):
        own = jnp.where(row == t, label_ref[t], own)
    hot_ref[...] = jnp.where(own == lax.broadcasted_iota(jnp.int32, (8, CLASSES), 1), 1.0, 0.0)


def pixel_box(v):
    lane = lax.broadcasted_iota(jnp.int32, v.shape, 1)
    col = lane & (SIDE - 1)
    v = v + jnp.where(col == 0, 0.0, pltpu.roll(v, 1, 1)) + jnp.where(col == SIDE - 1, 0.0, pltpu.roll(v, PIXELS - 1, 1))
    above = jnp.where(lane < SIDE, 0.0, pltpu.roll(v, SIDE, 1))
    below = jnp.where(lane >= PIXELS - SIDE, 0.0, pltpu.roll(v, PIXELS - SIDE, 1))
    return v + above + below


def spread_kernel(s0_ref, s1_ref, s2_ref, s3_ref, y_ref, rb_ref, sb_ref, q_ref, parts_ref):
    def keep(k, v):
        for i in range(ROWS):
            row = jnp.concatenate([v[:, q * 256 + i * SIDE : q * 256 + (i + 1) * SIDE] for q in range(4)], axis=1)
            for g in range(2):
                q_ref[k, (g * ROWS + i) * SG : (g * ROWS + i + 1) * SG] = row[g * SG : (g + 1) * SG]

    energy = None
    for c in range(3):
        image = jnp.concatenate([ref[c] for ref in (s0_ref, s1_ref, s2_ref, s3_ref)], axis=0)
        energy = image * image if energy is None else energy + image * image
        keep(c, image * (1.0 / 27.0))
    level = pixel_box(energy * (1.0 / 27.0)) + BETA
    for l in range(3):
        inverse = lax.rsqrt(level)
        keep(3 + l, inverse)
        if l < 2:
            level = pixel_box(level * (1.0 / 9.0)) + BETA

    first = lax.broadcasted_iota(jnp.int32, (DEEP * SG, 128), 1) // TG * SIDE
    image = q_ref[:3].reshape(3 * 128, 128)
    hi = image.astype(jnp.bfloat16)
    rest = image - hi.astype(F32)
    mid = rest.astype(jnp.bfloat16)
    low = (rest - mid.astype(F32)).astype(jnp.bfloat16)
    parts_ref[...] = jnp.concatenate([hi, mid, low], axis=1)
    row = lax.broadcasted_iota(jnp.int32, (128, 256), 0)
    lane = lax.broadcasted_iota(jnp.int32, (128, 256), 1)
    place = row - (lane & 127) // TG * SIDE - lax.shift_right_logical(lane, 7)

    def body(k, carry):
        pick = jnp.where(place == 2 * k, 1.0, 0.0).astype(jnp.bfloat16)
        both = jnp.dot(parts_ref[...], jnp.concatenate([pick] * 3, axis=0), preferred_element_type=F32)
        for n in range(2):
            j = 2 * k + n
            y_ref[:, pl.ds(j, 1)] = both[:, n * 128 : (n + 1) * 128].reshape(3, 1, DEEP, SG, 128)
            for l in range(3):
                one = jnp.take_along_axis(q_ref[3 + l], first + j, axis=1).reshape(1, DEEP, SG, 128)
                rb_ref[l, pl.ds(j, 1)] = one
                sb_ref[l, pl.ds(j, 1)] = lax.rsqrt(one * one) * (1.0 / 9.0)
        return carry

    lax.fori_loop(0, SIDE // 2, body, 0, unroll=4)


def spread(ref, k, j):
    return ref[k, pl.ds(j, 1)][0]


def own_duals(dual_ref):
    tgt = lax.axis_index("tgt")
    return [dual_ref[pl.ds((tgt ^ k) * 4, 4), :] for k in (0, 1, 8, 9)]


def block_rows(ref, r):
    z = lax.axis_index("tgt") // 2 % 4
    at_z = (z, z ^ 1, 3 - z, z ^ 2)[r]
    return ref.at[pl.ds(pl.multiple_of(at_z * 8, 8), 8), :]


def forward_kernel(
    x_ref, y_ref, rb_ref, sb_ref, dual_ref, hot_ref,
    pred_ref, xt_ref, h0_ref, h1_ref, w0_ref, w1_ref, w2_ref, v2_ref,
    ra_ref, sa_ref, va_ref, vb_ref,
):
    energy = None
    for c in range(3):
        parts = []
        for q in range(4):
            for r in range(4):
                parts.append(x_ref[r, c * 8 : (c + 1) * 8, q * 256 : (q + 1) * 256])
        turned = jnp.concatenate(parts, axis=0).T.reshape(ROWS, SIDE, 128)
        xt_ref[c] = turned
        energy = turned * turned if energy is None else energy + turned * turned
    level = target_box(energy * (1.0 / 27.0)) + BETA
    for l in range(3):
        inverse = lax.rsqrt(level)
        ra_ref[l] = inverse
        sa_ref[l] = level * inverse * (1.0 / math.pi)
        if l < 2:
            level = target_box(level * (1.0 / 9.0)) + BETA

    clear_edges(va_ref, vb_ref, v2_ref)

    def inner(j, carry):
        total = spread(y_ref, 0, j) * wide(xt_ref, 0, j)
        total = total + spread(y_ref, 1, j) * wide(xt_ref, 1, j)
        total = total + spread(y_ref, 2, j) * wide(xt_ref, 2, j)
        va_ref[pl.ds(j + 1, 1)] = down(total)[None]
        return carry

    lax.fori_loop(0, SIDE, inner, 0, unroll=2)

    def layer(l, j, around):
        cross = around + BETA
        x = cross * (spread(rb_ref, l, j) * wide(ra_ref, l, j))
        u = jnp.abs(x) if l == 0 else x
        d = jnp.maximum(1.0 - u * u, 1e-30)
        s = d * lax.rsqrt(d)
        top = (u * (TOP[2] / (9.0 * math.pi)) + TOP[1] / (9.0 * math.pi)) * u + TOP[0] / (9.0 * math.pi)
        q = s * (top * lax.rsqrt((u + BOTTOM[1]) * u + BOTTOM[0]))
        h = 1.0 / 9.0 - q
        if l == 0:
            h = jnp.where(x >= 0.0, h, q)
        w = (spread(sb_ref, l, j) * wide(sa_ref, l, j)) * s
        return h, w, w + h * cross

    def layer0(k, carry):
        for j, around in columns(va_ref, k):
            h, w, f = layer(0, j, around)
            h0_ref[pl.ds(j, 1)] = h[None]
            w0_ref[pl.ds(j, 1)] = w[None]
            vb_ref[pl.ds(j + 1, 1)] = down(f)[None]
        return carry

    def layer1(k, carry):
        for j, around in columns(vb_ref, k):
            h, w, f = layer(1, j, around)
            h1_ref[pl.ds(j, 1)] = h[None]
            w1_ref[pl.ds(j, 1)] = w[None]
            va_ref[pl.ds(j + 1, 1)] = down(f)[None]
        return carry

    def layer2(k, total):
        for j, around in columns(va_ref, k):
            h, w, f = layer(2, j, around)
            w2_ref[pl.ds(j, 1)] = w[None]
            v2_ref[pl.ds(j + 1, 1)] = down(h)[None]
            total = total + jnp.sum(f.reshape(2, ROWS, SG, 128), axis=1)
        return total

    lax.fori_loop(0, SIDE // 2, layer0, 0, unroll=2)
    lax.fori_loop(0, SIDE // 2, layer1, 0, unroll=2)
    total = lax.fori_loop(0, SIDE // 2, layer2, jnp.zeros((2, SG, 128), F32), unroll=2)
    kernel = total * (9.0 / PIXELS)
    duals = own_duals(dual_ref)
    wide_pred = None
    for g in range(2):
        part = lax.dot_general(
            kernel[g], jnp.concatenate(duals[2 * g : 2 * g + 2], axis=0), (((0,), (0,)), ((), ())),
            precision=lax.Precision.HIGHEST, preferred_element_type=F32,
        )
        wide_pred = part if wide_pred is None else wide_pred + part
    pred = wide_pred[:32] + wide_pred[32:64] + wide_pred[64:96] + wide_pred[96:]
    for r in range(4):
        rows = pred[r * 8 : (r + 1) * 8]
        if r == 0:
            rows = rows - jnp.where(lax.axis_index("sup") == 0, hot_ref[...], 0.0)
        block_rows(pred_ref, r)[...] = rows


def clear_edges(*refs):
    for ref in refs:
        ref[0] = jnp.zeros((DEEP, SG, 128), F32)
        ref[SIDE + 1] = jnp.zeros((DEEP, SG, 128), F32)


def at(ref, j):
    return ref[pl.ds(j, 1)][0]


def back_kernel_a(v2_ref, h1_ref, w1_ref, w2_ref, h0_ref, w0_ref, rb_ref, v0_ref, l0_ref, p1_ref, l1_ref, v1_ref, p2_ref):
    clear_edges(v1_ref, p2_ref, v0_ref, p1_ref)

    def layer1(k, carry):
        for j, up in columns(v2_ref, k):
            rb = spread(rb_ref, 1, j)
            l1_ref[pl.ds(j, 1)] = (up * at(w1_ref, j) * (rb * rb))[None]
            v1_ref[pl.ds(j + 1, 1)] = down(up * at(h1_ref, j))[None]
            rb = spread(rb_ref, 2, j)
            p2_ref[pl.ds(j + 1, 1)] = down(at(w2_ref, j) * (rb * rb))[None]
        return carry

    def layer0(k, carry):
        for (j, up), (_, sums) in zip(columns(v1_ref, k), columns(p2_ref, k)):
            rb = spread(rb_ref, 0, j)
            l0_ref[pl.ds(j, 1)] = (up * at(w0_ref, j) * (rb * rb))[None]
            v0_ref[pl.ds(j + 1, 1)] = down(up * at(h0_ref, j))[None]
            p1_ref[pl.ds(j + 1, 1)] = down(at(l1_ref, j) + sums * (1.0 / 9.0))[None]
        return carry

    lax.fori_loop(0, SIDE // 2, layer1, 0, unroll=2)
    lax.fori_loop(0, SIDE // 2, layer0, 0, unroll=2)


def back_kernel_b(l0_ref, p1_ref, p0_ref):
    clear_edges(p0_ref)

    def body(k, carry):
        for j, sums in columns(p1_ref, k):
            p0_ref[pl.ds(j + 1, 1)] = down(at(l0_ref, j) + sums * (1.0 / 9.0))[None]
        return carry

    lax.fori_loop(0, SIDE // 2, body, 0, unroll=2)


def back_kernel_c(v0_ref, p0_ref, xt_ref, y_ref, g_ref):
    def body(k, carry):
        for (j, up), (_, energy) in zip(columns(v0_ref, k), columns(p0_ref, k)):
            energy = energy * 27.0
            for c in range(3):
                g_ref[c, pl.ds(j, 1)] = (up * wide(xt_ref, c, j) + energy * spread(y_ref, c, j))[None]
        return carry

    lax.fori_loop(0, SIDE // 2, body, 0)


def sum_kernel(res_ref, dual_ref, g_ref, own_ref, *out_refs):
    own_ref[...] = block_rows(res_ref, 0)[...]
    rows = [block_rows(res_ref, r)[...] for r in range(4)]
    weight = lax.dot_general(
        jnp.concatenate(own_duals(dual_ref), axis=0) * (1.0 / 3.0), jnp.concatenate(rows * 4, axis=0), (((1,), (1,)), ((), ())),
        precision=lax.Precision.HIGHEST, preferred_element_type=F32,
    )
    weight = jnp.broadcast_to(weight.reshape(2, 1, SG, 128), (2, ROWS, SG, 128)).reshape(DEEP, SG, 128)
    row = lax.broadcasted_iota(jnp.int32, (512, 128), 0)
    col = lax.broadcasted_iota(jnp.int32, (512, 128), 1)
    place = col - (row & 127) // TG * SIDE - lax.shift_right_logical(row, 7)
    total = jnp.zeros((3 * 128, 128), F32)
    for j in range(0, SIDE, 4):
        pick = jnp.where(place == j, 1.0, 0.0).astype(jnp.bfloat16)
        his, lows = [], []
        for k in range(4):
            term = (g_ref[:, j + k] * weight).reshape(3 * 128, 128)
            hi = term.astype(jnp.bfloat16)
            his.append(hi)
            lows.append((term - hi.astype(F32)).astype(jnp.bfloat16))
        total = total + jnp.dot(jnp.concatenate(his, axis=1), pick, preferred_element_type=F32)
        total = total + jnp.dot(jnp.concatenate(lows, axis=1), pick, preferred_element_type=F32)
    for c in range(3):
        for g in range(2):
            image = [total[((c * 2 + g) * ROWS + i) * SG : ((c * 2 + g) * ROWS + i + 1) * SG] for i in range(ROWS)]
            line = jnp.concatenate([image[i][:, q * SIDE : (q + 1) * SIDE] for q in range(4) for i in range(ROWS)], axis=1)
            out_refs[0][c, g * 4 : g * 4 + 4] = line[:4]
            out_refs[1][c, g * 4 : g * 4 + 4] = line[4:]


def near(x):
    return pltpu.with_memory_space_constraint(x, pltpu.VMEM)


def vm(*shape):
    return pltpu.VMEM(shape, F32)


def hb(*shape):
    return jax.ShapeDtypeStruct(shape, F32)


def cost(mib):
    return pl.CostEstimate(flops=0, transcendentals=0, bytes_accessed=mib << 20)


def params(mib):
    return pltpu.CompilerParams(vmem_limit_bytes=mib << 20)


def shards(target_pool, target_index, target_labels, dual_weights, support_images):
    mine = support_images.transpose(1, 0, 2)
    across = send(mine, other_y)
    beside = send(mine, other_core)
    hbm = pl.BlockSpec(memory_space=pltpu.HBM)
    dma = pltpu.SemaphoreType.DMA(())
    pool = target_pool.transpose(1, 0, 2)
    block, duals, here, hot = pl.pallas_call(
        pick_kernel, out_shape=(vm(24, PIXELS), vm(*dual_weights.shape), vm(*mine.shape), vm(8, CLASSES)),
        in_specs=[hbm] * 5, out_specs=(VMEM,) * 4,
        scratch_shapes=[pltpu.SMEM((8,), jnp.int32), pltpu.SMEM((8,), jnp.int32), pltpu.VMEM(pool.shape, F32)] + [dma] * 5,
        compiler_params=params(4), name="pick", cost_estimate=cost(2),
    )(*[pltpu.with_memory_space_constraint(v, pltpu.HBM) for v in (target_index, target_labels, pool, dual_weights, mine)])
    block, beside = lax.optimization_barrier((block, beside))
    support = [here, beside, across, send(across, other_core)]
    x_all = jnp.stack([block, send(block, STEPS[0]), send(block, STEPS[1]), send(block, far_z)])
    spread_shape = (3, SIDE, DEEP, SG, 128)
    y_wide, rb_wide, sb_wide = pl.pallas_call(
        spread_kernel, out_shape=(vm(*spread_shape),) * 3, in_specs=[VMEM] * 4, out_specs=(VMEM,) * 3,
        scratch_shapes=[pltpu.VMEM((6, DEEP * SG, 128), F32), pltpu.VMEM((3 * 128, 3 * 128), jnp.bfloat16)], compiler_params=params(6), name="spread", cost_estimate=cost(12),
    )(*support)

    column = (SIDE, DEEP, SG, 128)
    padded = (SIDE + 2, DEEP, SG, 128)
    flat = (3, ROWS, SIDE, 128)

    def near_call(kernel, outs, ins, name, moved, scratch=(), mib=6):
        return pl.pallas_call(
            kernel, out_shape=tuple(vm(*o) for o in outs), in_specs=[VMEM] * len(ins), out_specs=(VMEM,) * len(outs),
            scratch_shapes=[pltpu.VMEM(v, F32) for v in scratch], compiler_params=params(mib), name=name, cost_estimate=cost(moved),
        )(*map(near, ins))

    pred, xt, h0, h1, w0, w1, w2, v2 = pl.pallas_call(
        forward_kernel,
        out_shape=(hb(TG, CLASSES), vm(*flat), vm(*column), vm(*column), vm(*column), vm(*column), vm(*column), vm(*padded)),
        in_specs=[VMEM] * 6,
        out_specs=(VMEM,) * 8,
        scratch_shapes=[pltpu.VMEM(flat, F32), pltpu.VMEM(flat, F32), pltpu.VMEM(padded, F32), pltpu.VMEM(padded, F32)],
        compiler_params=params(14), name="forward", cost_estimate=cost(32),
    )(x_all, near(y_wide), near(rb_wide), near(sb_wide), near(duals), near(hot))

    def around(res, moves):
        near_a, near_b, far = [send(res, move) for move in moves]
        return lambda: (res + near_a) + (near_b + far)

    res, v2 = lax.optimization_barrier((pred, v2))
    added = around(res, (STEPS[0], STEPS[1], far_z))
    v0, l0, p1 = near_call(
        back_kernel_a, (padded, column, padded), (v2, h1, w1, w2, h0, w0, rb_wide), "back_a", 8,
        scratch=(column, padded, padded), mib=9,
    )
    res, l0 = lax.optimization_barrier((added(), l0))
    new = send(res, STEPS[2])
    (p0,) = near_call(back_kernel_b, (padded,), (l0, p1), "back_b", 3)
    res, p0 = lax.optimization_barrier((res + new, p0))
    added = around(res, (STEPS[3], STEPS[4], far_x))
    (g,) = near_call(back_kernel_c, ((3,) + column,), (v0, p0, xt, y_wide), "back_c", 5)
    res = added()

    residual, *parts = pl.pallas_call(
        sum_kernel, out_shape=(hb(8, CLASSES),) + (hb(3, 8, PIXELS),) * 2,
        in_specs=[VMEM] * 3, out_specs=(VMEM,) * 3,
        compiler_params=params(10), name="weighted", cost_estimate=cost(10),
    )(res, near(duals), near(g))
    pair = parts[0] + send(parts[1], other_core)
    total = pair[:, :4] + send(pair[:, 4:], other_y)
    return (residual, total.transpose(1, 0, 2))


def solution(mesh):
    in_specs = (
        P("tgt", None, None),
        P("tgt"),
        P("tgt"),
        P("sup", None),
        P(("sup", "tgt"), None, None),
    )
    out_specs = (P("tgt", None), P(("sup", "tgt"), None, None))
    return jax.shard_map(shards, mesh=mesh, in_specs=in_specs, out_specs=out_specs, check_vma=False)
```

```python
import math

import jax
import jax.numpy as jnp
import numpy as np
from jax import lax
from jax.experimental import pallas as pl
from jax.experimental.pallas import tpu as pltpu
from jax.sharding import PartitionSpec as P

SIDE = 32
CLASSES = 100
PIXELS = 1024
BETA = 0.01
TG = 32
SG = 8
ROWS = 8
DEEP = 16
AXES = ("tgt", "sup")
DIMS = (2, 4, 2, 2, 4)

TOP = (2.4493771255467647, 0.1932864690474489, -0.013754684085600787)
BOTTOM = (2.431483473487932, 3.4797192205950016)

VMEM = pl.BlockSpec(memory_space=pltpu.VMEM)
SMEM = pl.BlockSpec(memory_space=pltpu.SMEM)
F32 = jnp.float32


def pairs_of(move):
    out = []
    for src in range(int(np.prod(DIMS))):
        at = [int(v) for v in np.unravel_index(src, DIMS)]
        out.append((src, int(np.ravel_multi_index(move(*at), DIMS))))
    return out


def send(x, move):
    return lax.ppermute(x, AXES, pairs_of(move))


def even(v):
    return v ^ 1


def odd(v):
    return 3 - v


STEPS = (
    lambda yh, z, c, yl, x: (yh, even(z), c, yl, x),
    lambda yh, z, c, yl, x: (yh, odd(z), c, yl, x),
    lambda yh, z, c, yl, x: (yh, z, c, 1 - yl, x),
    lambda yh, z, c, yl, x: (yh, z, c, yl, even(x)),
    lambda yh, z, c, yl, x: (yh, z, c, yl, odd(x)),
)


def far_z(yh, z, c, yl, x):
    return (yh, z ^ 2, c, yl, x)


def far_x(yh, z, c, yl, x):
    return (yh, z, c, yl, x ^ 2)


def other_core(yh, z, c, yl, x):
    return (yh, z, 1 - c, yl, x)


def other_y(yh, z, c, yl, x):
    return (1 - yh, z, c, yl, x)


def rows_sum(v):
    lane = lax.broadcasted_iota(jnp.int32, v.shape[1:], 1)
    above = jnp.where(lane >= TG, pltpu.roll(v[ROWS - 1], TG, 1), 0.0)
    below = jnp.where(lane < 128 - TG, pltpu.roll(v[0], 128 - TG, 1), 0.0)
    line = [above] + [v[i] for i in range(ROWS)] + [below]
    out = []
    for i in range(1, ROWS + 1, 2):
        both = line[i] + line[i + 1]
        out += [line[i - 1] + both, both + line[i + 2]]
    return jnp.stack(out)


def down(v):
    return jnp.concatenate([rows_sum(v[:ROWS]), rows_sum(v[ROWS:])], axis=0)


def target_box(v):
    col = lax.broadcasted_iota(jnp.int32, v.shape, 1)
    v = v + jnp.where(col == 0, 0.0, pltpu.roll(v, 1, 1)) + jnp.where(col == SIDE - 1, 0.0, pltpu.roll(v, SIDE - 1, 1))
    return rows_sum(v)


def columns(ref, k):
    first, left, right, last = [ref[pl.ds(2 * k + n, 1)][0] for n in range(4)]
    both = left + right
    return ((2 * k, first + both), (2 * k + 1, both + last))


def wide(ref, k, j):
    one = jnp.broadcast_to(ref[k, :, pl.ds(j, 1), :], (ROWS, SG, 128))
    return jnp.concatenate([one, one], axis=0)


def pick_kernel(
    index_hbm, label_hbm, pool_hbm, dual_hbm, mine_hbm, block_ref, dual_ref, mine_ref, hot_ref,
    index_ref, label_ref, pool_ref, index_sem, label_sem, pool_sem, dual_sem, mine_sem,
):
    copies = [
        pltpu.make_async_copy(index_hbm, index_ref, index_sem),
        pltpu.make_async_copy(pool_hbm, pool_ref, pool_sem),
        pltpu.make_async_copy(label_hbm, label_ref, label_sem),
        pltpu.make_async_copy(dual_hbm, dual_ref, dual_sem),
        pltpu.make_async_copy(mine_hbm, mine_ref, mine_sem),
    ]
    for copy in copies:
        copy.start()
    for copy in copies:
        copy.wait()
    base = lax.axis_index("tgt") * pool_ref.shape[1]
    for t in range(8):
        one = pool_ref[:, pl.ds(index_ref[t] - base, 1), :]
        for c in range(3):
            block_ref[c * 8 + t : c * 8 + t + 1] = one[c]
    row = lax.broadcasted_iota(jnp.int32, (8, CLASSES), 0)
    own = jnp.zeros((8, CLASSES), jnp.int32)
    for t in range(8):
        own = jnp.where(row == t, label_ref[t], own)
    hot_ref[...] = jnp.where(own == lax.broadcasted_iota(jnp.int32, (8, CLASSES), 1), 1.0, 0.0)


def pixel_box(v):
    lane = lax.broadcasted_iota(jnp.int32, v.shape, 1)
    col = lane & (SIDE - 1)
    v = v + jnp.where(col == 0, 0.0, pltpu.roll(v, 1, 1)) + jnp.where(col == SIDE - 1, 0.0, pltpu.roll(v, PIXELS - 1, 1))
    above = jnp.where(lane < SIDE, 0.0, pltpu.roll(v, SIDE, 1))
    below = jnp.where(lane >= PIXELS - SIDE, 0.0, pltpu.roll(v, PIXELS - SIDE, 1))
    return v + above + below


def spread_kernel(s0_ref, s1_ref, s2_ref, s3_ref, y_ref, rb_ref, sb_ref, q_ref, parts_ref):
    def keep(k, v):
        for i in range(ROWS):
            row = jnp.concatenate([v[:, q * 256 + i * SIDE : q * 256 + (i + 1) * SIDE] for q in range(4)], axis=1)
            for g in range(2):
                q_ref[k, (g * ROWS + i) * SG : (g * ROWS + i + 1) * SG] = row[g * SG : (g + 1) * SG]

    energy = None
    for c in range(3):
        image = jnp.concatenate([ref[c] for ref in (s0_ref, s1_ref, s2_ref, s3_ref)], axis=0)
        energy = image * image if energy is None else energy + image * image
        keep(c, image * (1.0 / 27.0))
    level = pixel_box(energy * (1.0 / 27.0)) + BETA
    for l in range(3):
        inverse = lax.rsqrt(level)
        keep(3 + l, inverse)
        if l < 2:
            level = pixel_box(level * (1.0 / 9.0)) + BETA

    first = lax.broadcasted_iota(jnp.int32, (DEEP * SG, 128), 1) // TG * SIDE
    image = q_ref[:3].reshape(3 * 128, 128)
    hi = image.astype(jnp.bfloat16)
    rest = image - hi.astype(F32)
    mid = rest.astype(jnp.bfloat16)
    low = (rest - mid.astype(F32)).astype(jnp.bfloat16)
    parts_ref[...] = jnp.concatenate([hi, mid, low], axis=1)
    row = lax.broadcasted_iota(jnp.int32, (128, 256), 0)
    lane = lax.broadcasted_iota(jnp.int32, (128, 256), 1)
    place = row - (lane & 127) // TG * SIDE - lax.shift_right_logical(lane, 7)

    def body(k, carry):
        pick = jnp.where(place == 2 * k, 1.0, 0.0).astype(jnp.bfloat16)
        both = jnp.dot(parts_ref[...], jnp.concatenate([pick] * 3, axis=0), preferred_element_type=F32)
        for n in range(2):
            j = 2 * k + n
            y_ref[:, pl.ds(j, 1)] = both[:, n * 128 : (n + 1) * 128].reshape(3, 1, DEEP, SG, 128)
            for l in range(3):
                one = jnp.take_along_axis(q_ref[3 + l], first + j, axis=1).reshape(1, DEEP, SG, 128)
                rb_ref[l, pl.ds(j, 1)] = one
                sb_ref[l, pl.ds(j, 1)] = lax.rsqrt(one * one) * (1.0 / 9.0)
        return carry

    lax.fori_loop(0, SIDE // 2, body, 0, unroll=4)


def spread(ref, k, j):
    return ref[k, pl.ds(j, 1)][0]


def own_duals(dual_ref):
    tgt = lax.axis_index("tgt")
    return [dual_ref[pl.ds((tgt ^ k) * 4, 4), :] for k in (0, 1, 8, 9)]


def block_rows(ref, r):
    z = lax.axis_index("tgt") // 2 % 4
    at_z = (z, z ^ 1, 3 - z, z ^ 2)[r]
    return ref.at[pl.ds(pl.multiple_of(at_z * 8, 8), 8), :]


def forward_kernel(
    x_ref, y_ref, rb_ref, sb_ref, dual_ref, hot_ref,
    pred_ref, xt_ref, h0_ref, h1_ref, w0_ref, w1_ref, w2_ref, v2_ref,
    ra_ref, sa_ref, va_ref, vb_ref,
):
    energy = None
    for c in range(3):
        parts = []
        for q in range(4):
            for r in range(4):
                parts.append(x_ref[r, c * 8 : (c + 1) * 8, q * 256 : (q + 1) * 256])
        turned = jnp.concatenate(parts, axis=0).T.reshape(ROWS, SIDE, 128)
        xt_ref[c] = turned
        energy = turned * turned if energy is None else energy + turned * turned
    level = target_box(energy * (1.0 / 27.0)) + BETA
    for l in range(3):
        inverse = lax.rsqrt(level)
        ra_ref[l] = inverse
        sa_ref[l] = level * inverse * (1.0 / math.pi)
        if l < 2:
            level = target_box(level * (1.0 / 9.0)) + BETA

    clear_edges(va_ref, vb_ref, v2_ref)

    def inner(j, carry):
        total = spread(y_ref, 0, j) * wide(xt_ref, 0, j)
        total = total + spread(y_ref, 1, j) * wide(xt_ref, 1, j)
        total = total + spread(y_ref, 2, j) * wide(xt_ref, 2, j)
        va_ref[pl.ds(j + 1, 1)] = down(total)[None]
        return carry

    lax.fori_loop(0, SIDE, inner, 0, unroll=2)

    def layer(l, j, around):
        cross = around + BETA
        x = cross * (spread(rb_ref, l, j) * wide(ra_ref, l, j))
        u = jnp.abs(x) if l == 0 else x
        d = jnp.maximum(1.0 - u * u, 1e-30)
        s = d * lax.rsqrt(d)
        top = (u * (TOP[2] / (9.0 * math.pi)) + TOP[1] / (9.0 * math.pi)) * u + TOP[0] / (9.0 * math.pi)
        q = s * (top * lax.rsqrt((u + BOTTOM[1]) * u + BOTTOM[0]))
        h = 1.0 / 9.0 - q
        if l == 0:
            h = jnp.where(x >= 0.0, h, q)
        w = (spread(sb_ref, l, j) * wide(sa_ref, l, j)) * s
        return h, w, w + h * cross

    def layer0(k, carry):
        for j, around in columns(va_ref, k):
            h, w, f = layer(0, j, around)
            h0_ref[pl.ds(j, 1)] = h[None]
            w0_ref[pl.ds(j, 1)] = w[None]
            vb_ref[pl.ds(j + 1, 1)] = down(f)[None]
        return carry

    def layer1(k, carry):
        for j, around in columns(vb_ref, k):
            h, w, f = layer(1, j, around)
            h1_ref[pl.ds(j, 1)] = h[None]
            w1_ref[pl.ds(j, 1)] = w[None]
            va_ref[pl.ds(j + 1, 1)] = down(f)[None]
        return carry

    def layer2(k, total):
        for j, around in columns(va_ref, k):
            h, w, f = layer(2, j, around)
            w2_ref[pl.ds(j, 1)] = w[None]
            v2_ref[pl.ds(j + 1, 1)] = down(h)[None]
            total = total + jnp.sum(f.reshape(2, ROWS, SG, 128), axis=1)
        return total

    lax.fori_loop(0, SIDE // 2, layer0, 0, unroll=2)
    lax.fori_loop(0, SIDE // 2, layer1, 0, unroll=2)
    total = lax.fori_loop(0, SIDE // 2, layer2, jnp.zeros((2, SG, 128), F32), unroll=2)
    kernel = total * (9.0 / PIXELS)
    duals = own_duals(dual_ref)
    wide_pred = None
    for g in range(2):
        part = lax.dot_general(
            kernel[g], jnp.concatenate(duals[2 * g : 2 * g + 2], axis=0), (((0,), (0,)), ((), ())),
            precision=lax.Precision.HIGHEST, preferred_element_type=F32,
        )
        wide_pred = part if wide_pred is None else wide_pred + part
    pred = wide_pred[:32] + wide_pred[32:64] + wide_pred[64:96] + wide_pred[96:]
    for r in range(4):
        rows = pred[r * 8 : (r + 1) * 8]
        if r == 0:
            rows = rows - jnp.where(lax.axis_index("sup") == 0, hot_ref[...], 0.0)
        block_rows(pred_ref, r)[...] = rows


def clear_edges(*refs):
    for ref in refs:
        ref[0] = jnp.zeros((DEEP, SG, 128), F32)
        ref[SIDE + 1] = jnp.zeros((DEEP, SG, 128), F32)


def at(ref, j):
    return ref[pl.ds(j, 1)][0]


def back_kernel_a(v2_ref, h1_ref, w1_ref, w2_ref, rb_ref, l1_ref, v1_ref, p2_ref):
    clear_edges(v1_ref, p2_ref)

    def layer1(k, carry):
        for j, up in columns(v2_ref, k):
            rb = spread(rb_ref, 1, j)
            l1_ref[pl.ds(j, 1)] = (up * at(w1_ref, j) * (rb * rb))[None]
            v1_ref[pl.ds(j + 1, 1)] = down(up * at(h1_ref, j))[None]
            rb = spread(rb_ref, 2, j)
            p2_ref[pl.ds(j + 1, 1)] = down(at(w2_ref, j) * (rb * rb))[None]
        return carry

    lax.fori_loop(0, SIDE // 2, layer1, 0, unroll=2)


def back_kernel_b(v1_ref, h0_ref, w0_ref, l1_ref, p2_ref, rb_ref, v0_ref, p0_ref, l0_ref, p1_ref):
    clear_edges(v0_ref, p1_ref, p0_ref)

    def layer0(k, carry):
        for (j, up), (_, sums) in zip(columns(v1_ref, k), columns(p2_ref, k)):
            rb = spread(rb_ref, 0, j)
            l0_ref[pl.ds(j, 1)] = (up * at(w0_ref, j) * (rb * rb))[None]
            v0_ref[pl.ds(j + 1, 1)] = down(up * at(h0_ref, j))[None]
            p1_ref[pl.ds(j + 1, 1)] = down(at(l1_ref, j) + sums * (1.0 / 9.0))[None]
        return carry

    def last(k, carry):
        for j, sums in columns(p1_ref, k):
            p0_ref[pl.ds(j + 1, 1)] = down(at(l0_ref, j) + sums * (1.0 / 9.0))[None]
        return carry

    lax.fori_loop(0, SIDE // 2, layer0, 0, unroll=2)
    lax.fori_loop(0, SIDE // 2, last, 0, unroll=2)


def back_kernel_c(v0_ref, p0_ref, xt_ref, y_ref, g_ref):
    def body(k, carry):
        for (j, up), (_, energy) in zip(columns(v0_ref, k), columns(p0_ref, k)):
            energy = energy * 27.0
            for c in range(3):
                g_ref[c, pl.ds(j, 1)] = (up * wide(xt_ref, c, j) + energy * spread(y_ref, c, j))[None]
        return carry

    lax.fori_loop(0, SIDE // 2, body, 0)


def sum_kernel(res_ref, dual_ref, g_ref, own_ref, *out_refs):
    own_ref[...] = block_rows(res_ref, 0)[...]
    rows = [block_rows(res_ref, r)[...] for r in range(4)]
    weight = lax.dot_general(
        jnp.concatenate(own_duals(dual_ref), axis=0) * (1.0 / 3.0), jnp.concatenate(rows * 4, axis=0), (((1,), (1,)), ((), ())),
        precision=lax.Precision.HIGHEST, preferred_element_type=F32,
    )
    weight = jnp.broadcast_to(weight.reshape(2, 1, SG, 128), (2, ROWS, SG, 128)).reshape(DEEP, SG, 128)
    row = lax.broadcasted_iota(jnp.int32, (512, 128), 0)
    col = lax.broadcasted_iota(jnp.int32, (512, 128), 1)
    place = col - (row & 127) // TG * SIDE - lax.shift_right_logical(row, 7)
    total = jnp.zeros((3 * 128, 128), F32)
    for j in range(0, SIDE, 4):
        pick = jnp.where(place == j, 1.0, 0.0).astype(jnp.bfloat16)
        his, lows = [], []
        for k in range(4):
            term = (g_ref[:, j + k] * weight).reshape(3 * 128, 128)
            hi = term.astype(jnp.bfloat16)
            his.append(hi)
            lows.append((term - hi.astype(F32)).astype(jnp.bfloat16))
        total = total + jnp.dot(jnp.concatenate(his, axis=1), pick, preferred_element_type=F32)
        total = total + jnp.dot(jnp.concatenate(lows, axis=1), pick, preferred_element_type=F32)
    for c in range(3):
        for g in range(2):
            image = [total[((c * 2 + g) * ROWS + i) * SG : ((c * 2 + g) * ROWS + i + 1) * SG] for i in range(ROWS)]
            line = jnp.concatenate([image[i][:, q * SIDE : (q + 1) * SIDE] for q in range(4) for i in range(ROWS)], axis=1)
            out_refs[0][c, g * 4 : g * 4 + 4] = line[:4]
            out_refs[1][c, g * 4 : g * 4 + 4] = line[4:]


def near(x):
    return pltpu.with_memory_space_constraint(x, pltpu.VMEM)


def vm(*shape):
    return pltpu.VMEM(shape, F32)


def hb(*shape):
    return jax.ShapeDtypeStruct(shape, F32)


def cost(mib):
    return pl.CostEstimate(flops=0, transcendentals=0, bytes_accessed=mib << 20)


def params(mib):
    return pltpu.CompilerParams(vmem_limit_bytes=mib << 20)


def shards(target_pool, target_index, target_labels, dual_weights, support_images):
    mine = support_images.transpose(1, 0, 2)
    across = send(mine, other_y)
    beside = send(mine, other_core)
    hbm = pl.BlockSpec(memory_space=pltpu.HBM)
    dma = pltpu.SemaphoreType.DMA(())
    pool = target_pool.transpose(1, 0, 2)
    block, duals, here, hot = pl.pallas_call(
        pick_kernel, out_shape=(vm(24, PIXELS), vm(*dual_weights.shape), vm(*mine.shape), vm(8, CLASSES)),
        in_specs=[hbm] * 5, out_specs=(VMEM,) * 4,
        scratch_shapes=[pltpu.SMEM((8,), jnp.int32), pltpu.SMEM((8,), jnp.int32), pltpu.VMEM(pool.shape, F32)] + [dma] * 5,
        compiler_params=params(4), name="pick", cost_estimate=cost(2),
    )(*[pltpu.with_memory_space_constraint(v, pltpu.HBM) for v in (target_index, target_labels, pool, dual_weights, mine)])
    block, beside = lax.optimization_barrier((block, beside))
    support = [here, beside, across, send(across, other_core)]
    x_all = jnp.stack([block, send(block, STEPS[0]), send(block, STEPS[1]), send(block, far_z)])
    spread_shape = (3, SIDE, DEEP, SG, 128)
    y_wide, rb_wide, sb_wide = pl.pallas_call(
        spread_kernel, out_shape=(vm(*spread_shape),) * 3, in_specs=[VMEM] * 4, out_specs=(VMEM,) * 3,
        scratch_shapes=[pltpu.VMEM((6, DEEP * SG, 128), F32), pltpu.VMEM((3 * 128, 3 * 128), jnp.bfloat16)], compiler_params=params(6), name="spread", cost_estimate=cost(12),
    )(*support)

    column = (SIDE, DEEP, SG, 128)
    padded = (SIDE + 2, DEEP, SG, 128)
    flat = (3, ROWS, SIDE, 128)

    def near_call(kernel, outs, ins, name, moved, scratch=(), mib=6):
        return pl.pallas_call(
            kernel, out_shape=tuple(vm(*o) for o in outs), in_specs=[VMEM] * len(ins), out_specs=(VMEM,) * len(outs),
            scratch_shapes=[pltpu.VMEM(v, F32) for v in scratch], compiler_params=params(mib), name=name, cost_estimate=cost(moved),
        )(*map(near, ins))

    pred, xt, h0, h1, w0, w1, w2, v2 = pl.pallas_call(
        forward_kernel,
        out_shape=(hb(TG, CLASSES), vm(*flat), vm(*column), vm(*column), vm(*column), vm(*column), vm(*column), vm(*padded)),
        in_specs=[VMEM] * 6,
        out_specs=(VMEM,) * 8,
        scratch_shapes=[pltpu.VMEM(flat, F32), pltpu.VMEM(flat, F32), pltpu.VMEM(padded, F32), pltpu.VMEM(padded, F32)],
        compiler_params=params(14), name="forward", cost_estimate=cost(32),
    )(x_all, near(y_wide), near(rb_wide), near(sb_wide), near(duals), near(hot))

    def around(res, moves):
        near_a, near_b, far = [send(res, move) for move in moves]
        return lambda: (res + near_a) + (near_b + far)

    res, v2 = lax.optimization_barrier((pred, v2))
    added = around(res, (STEPS[0], STEPS[1], far_z))
    l1, v1, p2 = near_call(back_kernel_a, (column, padded, padded), (v2, h1, w1, w2, rb_wide), "back_a", 5)
    res, v1 = lax.optimization_barrier((added(), v1))
    new = send(res, STEPS[2])
    v0, p0 = near_call(
        back_kernel_b, (padded, padded), (v1, h0, w0, l1, p2, rb_wide), "back_b", 6,
        scratch=(column, padded), mib=7,
    )
    res, p0 = lax.optimization_barrier((res + new, p0))
    added = around(res, (STEPS[3], STEPS[4], far_x))
    (g,) = near_call(back_kernel_c, ((3,) + column,), (v0, p0, xt, y_wide), "back_c", 5)
    res = added()

    residual, *parts = pl.pallas_call(
        sum_kernel, out_shape=(hb(8, CLASSES),) + (hb(3, 8, PIXELS),) * 2,
        in_specs=[VMEM] * 3, out_specs=(VMEM,) * 3,
        compiler_params=params(10), name="weighted", cost_estimate=cost(10),
    )(res, near(duals), near(g))
    pair = parts[0] + send(parts[1], other_core)
    total = pair[:, :4] + send(pair[:, 4:], other_y)
    return (residual, total.transpose(1, 0, 2))


def solution(mesh):
    in_specs = (
        P("tgt", None, None),
        P("tgt"),
        P("tgt"),
        P("sup", None),
        P(("sup", "tgt"), None, None),
    )
    out_specs = (P("tgt", None), P(("sup", "tgt"), None, None))
    return jax.shard_map(shards, mesh=mesh, in_specs=in_specs, out_specs=out_specs, check_vma=False)
```
